128 devices in a mesh: dp: 16 (over x, y), mp: 8 (over z, core).
Axes of the slice: x: 4, y: 4, z: 4, core: 2. Of those that a mesh axis runs over, the one named last changes fastest.
Arguments:
- tokens: bfloat16 [6144, 8192], P('dp', 'mp'), may hold values from -6 to 6
- cotangent: bfloat16 [6144, 8192], P('dp', 'mp'), may hold values from -1.5 to 1.5
- token_adapter_index: int32 [6144, 1], P('dp'), may hold values from 0 to 127; in each aligned block of 384 rows (0 to 383, 384 to 767, ...) at most 6 rows name the same one
- adapter_storage_row: int32 [128], replicated, may hold values from 0 to 127, each once
- frozen_weight_matrix: bfloat16 [8192, 8192], P(None, 'mp'), may hold values from -0.0625 to 0.0625
- first_adapter_factors: bfloat16 [128, 64, 8192], P('dp', None, 'mp'), may hold values from -0.0625 to 0.0625
- second_adapter_factors: bfloat16 [128, 64, 8192], P('dp', None, 'mp'), may hold values from -0.0625 to 0.0625
Outputs:
- output: bfloat16 [6144, 8192], P('dp', 'mp')
- input_gradient: bfloat16 [6144, 8192], P(('dp', 'mp'))
- first_factor_gradient: float32 [128, 64, 8192], P('dp', None, 'mp')
- second_factor_gradient: float32 [128, 64, 8192], P('dp', None, 'mp')
The draws below stay inside these ranges and needn't reach their ends.
Inputs may be any that keep to these rules, and one draw needn't show every extreme that they name: `token_adapter_index`: in the rows of one device no adapter is named by more than 6 rows, a bound that some block reaches. `adapter_storage_row`: each adapter has its own storage row.
All inputs are finite; a program needn't handle non-finite values.
Results may differ from the reference program's by a relative error of at most 0.019.
Values may be sent and summed in bfloat16 or wider, within the bound.
A program may use at most 128 MiB of HBM per device.

```python
import math
import jax
import jax.numpy as jnp
import numpy as np
from jax import lax

MODEL_WIDTH = 8192
ADAPTER_RANK = 64
TOK_DEV = 384
ADAPTER_TOTAL = 128
CAP = 6
TOKENS = 6144
N_DP = 16
N_MP = 8


def block_scale(stream_key, extent, cuts, smallest, high):
    level, own = 1.0, jax.random.fold_in(stream_key, 6)
    for axis_at, parts in cuts:
        draws = jnp.exp(jax.random.uniform(jax.random.fold_in(own, axis_at), (parts,), jnp.float32, smallest / len(cuts), high / len(cuts)))
        level = level * jnp.repeat(draws, extent[axis_at] // parts).reshape([-1 if axis == axis_at else 1 for axis in range(len(extent))])
    return level


def shared_out(key, own, number, rows, count, top, most, lean):
    sequence = jax.random.permutation(key, count)
    crowded, ordinary = portions_of(count, rows * top, most, lean, True), portions_of(count, rows * top, most, lean, False)
    places = jnp.arange(count)

    def named(tallies, rotation):
        used = int((tallies > 0).sum())
        fixed = max(1, used // 4)
        passed = fixed + (places - fixed + rotation * (used - fixed)) % max(1, count - fixed)
        return jnp.zeros((count,), jnp.int32).at[sequence[jnp.where(places < fixed, places, passed)]].set(jnp.asarray(tallies, jnp.int32))

    tallies = jnp.where(number % 4 == 0, named(crowded, number // 4), named(ordinary, number - number // 4 - 1))
    mixed = jax.random.permutation(jax.random.fold_in(own, 3), count)
    donor, sink = mixed[0:count // 2 * 2:2], mixed[1:count // 2 * 2:2]
    slack = jnp.minimum(tallies[donor] - 1, most - tallies[sink]) // 2
    slack = jnp.where((donor == sequence[0]) | (sink == sequence[0]) | (tallies[sink] == 0), 0, jnp.maximum(slack, 0))
    passed = jax.random.randint(jax.random.fold_in(own, 4), (count // 2,), 0, 1 << 20) % (slack + 1)
    tallies = tallies.at[donor].add(-passed).at[sink].add(passed)
    items = jnp.searchsorted(jnp.cumsum(tallies), jnp.arange(rows * top), side="right").astype(jnp.int32)
    listing = items.reshape(top, rows).T
    listing = listing[jax.random.permutation(jax.random.fold_in(own, 1), rows)]
    rotation = jax.random.randint(jax.random.fold_in(own, 2), (rows, 1), 0, top)
    return jnp.take_along_axis(listing, (jnp.arange(top)[None, :] + rotation) % top, axis=1)


def portions_of(count, total, most, slope, full):
    loads = [(1 << 20) // math.isqrt(grade ** slope) + 1 for grade in range(1, count + 1)]
    largest = most if full else min(most, max(-(-total // count), total * loads[0] // sum(loads)))
    least = 1 if total - largest >= count - 1 else 0
    counts, surplus = [largest] + [least] * (count - 1), total - largest - least * (count - 1)
    while surplus > 0:
        candidates = [i for i in range(1, count) if counts[i] < largest] or [i for i in range(1, count) if counts[i] < most]
        pool, left = sum([loads[i] for i in candidates]), surplus
        for i in candidates:
            more = min(most - counts[i], max(1, left * loads[i] // pool), surplus)
            counts[i] = counts[i] + more
            surplus = surplus - more
    return np.array(counts)


def scatter_about(stream_key, extent, width, limit, split=(), held_as=jnp.bfloat16):
    drawn = jax.random.normal(stream_key, extent, jnp.float32) * width
    if len(split) > 0:
        drawn = block_scale(stream_key, extent, split, -0.22, 0.18) * drawn
    return jnp.clip(drawn, min=-limit, max=limit).astype(held_as)


def setup_inputs(seed: int = 0) -> dict:
    splits = jax.random.split(jax.random.key(seed), 8)
    tokens = scatter_about(splits[0], (TOKENS, MODEL_WIDTH), 1.0, 6.0, ((0, 16), (1, 8)))
    cotangent = scatter_about(splits[1], (TOKENS, MODEL_WIDTH), 0.25, 1.5, ((0, 16), (1, 8)))
    token_adapter_index_keys = jax.random.split(jax.random.fold_in(splits[2], 1), TOKENS // TOK_DEV)
    token_adapter_index_turns = jax.random.permutation(jax.random.fold_in(splits[2], 3), TOKENS // TOK_DEV)
    token_adapter_index = jax.vmap(lambda own, number: shared_out(jax.random.fold_in(splits[2], 2), own, number, TOK_DEV, ADAPTER_TOTAL, 1, CAP, 2))(token_adapter_index_keys, token_adapter_index_turns).reshape((TOKENS, 1))
    adapter_storage_row = jax.random.permutation(splits[3], ADAPTER_TOTAL).astype(jnp.int32)
    frozen_weight_matrix = scatter_about(splits[4], (MODEL_WIDTH, MODEL_WIDTH), MODEL_WIDTH ** -0.5, 0.0625, ((1, 8),))
    first_adapter_factors = scatter_about(splits[5], (ADAPTER_TOTAL, ADAPTER_RANK, MODEL_WIDTH), MODEL_WIDTH ** -0.5, 0.0625, ((0, 16), (2, 8)))
    second_adapter_factors = scatter_about(splits[6], (ADAPTER_TOTAL, ADAPTER_RANK, MODEL_WIDTH), MODEL_WIDTH ** -0.5, 0.0625, ((0, 16), (2, 8)))
    return dict(tokens=tokens, cotangent=cotangent, token_adapter_index=token_adapter_index, adapter_storage_row=adapter_storage_row, frozen_weight_matrix=frozen_weight_matrix, first_adapter_factors=first_adapter_factors, second_adapter_factors=second_adapter_factors)


adapter_scale = 2.0


def reference(tokens, cotangent, token_adapter_index, adapter_storage_row, frozen_weight_matrix, first_adapter_factors, second_adapter_factors):
    token_count = tokens.shape[0]
    storage = adapter_storage_row[token_adapter_index[:, 0]]
    onehot = (storage[:, None] == jnp.arange(ADAPTER_TOTAL, dtype=jnp.int32)[None, :]).astype(jnp.int32)
    position = jnp.sum((jnp.cumsum(onehot, axis=0) - onehot) * onehot, axis=1).astype(jnp.int32)
    most = CAP * N_DP
    table = jnp.full((ADAPTER_TOTAL, most), token_count, jnp.int32)
    table = table.at[storage, position].set(jnp.arange(token_count, dtype=jnp.int32))
    padded_x = jnp.concatenate([tokens, jnp.zeros((1, MODEL_WIDTH), tokens.dtype)], axis=0)
    padded_g = jnp.concatenate([cotangent, jnp.zeros((1, MODEL_WIDTH), cotangent.dtype)], axis=0)

    def grouped_by_adapter(position_index):
        picked = table[position_index]
        input_row_values = padded_x[picked]
        gradient_row_values = padded_g[picked]
        first_factor = first_adapter_factors[position_index]
        second_factor = second_adapter_factors[position_index]
        down_rank_values = jnp.dot(input_row_values, first_factor.T, preferred_element_type=jnp.float32).astype(jnp.bfloat16)
        gradient_rank_values = jnp.dot(gradient_row_values, second_factor.T, preferred_element_type=jnp.float32).astype(jnp.bfloat16)
        adapter_output = (adapter_scale * jnp.dot(down_rank_values, second_factor, preferred_element_type=jnp.float32)).astype(jnp.bfloat16)
        adapter_backward = (adapter_scale * jnp.dot(gradient_rank_values, first_factor, preferred_element_type=jnp.float32)).astype(jnp.bfloat16)
        single_second_gradient = adapter_scale * jnp.dot(down_rank_values.T, gradient_row_values, preferred_element_type=jnp.float32)
        single_first_gradient = adapter_scale * jnp.dot(gradient_rank_values.T, input_row_values, preferred_element_type=jnp.float32)
        return adapter_output, adapter_backward, single_first_gradient, single_second_gradient

    adapter_output, adapter_backward, first_factor_gradient, second_factor_gradient = lax.map(grouped_by_adapter, jnp.arange(ADAPTER_TOTAL, dtype=jnp.int32))
    flattened_values = table.reshape(-1)
    output_adapter_term = jnp.zeros((token_count + 1, MODEL_WIDTH), jnp.float32).at[flattened_values].add(adapter_output.reshape(-1, MODEL_WIDTH).astype(jnp.float32))[:token_count]
    backward_adapter_term = jnp.zeros((token_count + 1, MODEL_WIDTH), jnp.float32).at[flattened_values].add(adapter_backward.reshape(-1, MODEL_WIDTH).astype(jnp.float32))[:token_count]
    output = (jnp.dot(tokens, frozen_weight_matrix, preferred_element_type=jnp.float32) + output_adapter_term).astype(jnp.bfloat16)
    block = MODEL_WIDTH // N_MP
    frozen_backward = jnp.zeros((token_count, MODEL_WIDTH), jnp.float32)
    for part in range(N_MP):
        cot_block = cotangent[:, part * block:(part + 1) * block]
        weight_block = frozen_weight_matrix[:, part * block:(part + 1) * block]
        partial_sum = lax.dot_general(cot_block, weight_block, (((1,), (1,)), ((), ())), preferred_element_type=jnp.float32)
        frozen_backward = frozen_backward + partial_sum.astype(jnp.bfloat16).astype(jnp.float32)
    input_gradient = (frozen_backward + backward_adapter_term).astype(jnp.bfloat16)
    return output, input_gradient, first_factor_gradient, second_factor_gradient
```

```python
import jax
import jax.numpy as jnp
from jax import lax
from jax.experimental import pallas as pl
from jax.experimental.pallas import tpu as pltpu
from jax.sharding import PartitionSpec as P

adapter_scale = 2.0
MESH = pl.DeviceIdType.MESH
bf16, f32, i32 = jnp.bfloat16, jnp.float32, jnp.int32

OFFSETS = (
    (1, 0), (3, 0), (0, 1), (0, 3), (2, 2), (1, 1), (3, 3), (1, 3),
    (3, 1), (2, 0), (0, 2), (2, 1), (1, 2), (2, 3), (3, 2),
)
NT = (((1,), (1,)), ((), ()))
TN = (((0,), (0,)), ((), ()))


def dot(a, b, dims=(((1,), (0,)), ((), ()))):
    return lax.dot_general(a, b, dims, preferred_element_type=f32)


def kernel(
    idx_ref, row_ref, tok_hbm, cot_hbm, w_hbm, a_hbm, b_hbm,
    out_hbm, ig_hbm, da_hbm, db_hbm,
    wv, xall, cot, av, bv, pt, pm, sendg, sendx, recvg, recvx, retb, reto,
    part, pr, r1, r2m, r2p, lbs, lbr, vsg, vrg, fing, vsx, vrx, finx, dg, dx, acc,
    grad, outb, igb,
    wsem, lsem, osem, ag_s, ag_r, g_s, g_r, x_s, x_r, rb_s, rb_r, ro_s, ro_r,
    p_s, p_r, z_s, z_r, agr_s, agr_r, axr_s, axr_r, lb_s, lb_r,
):
    s, m = lax.axis_index("dp"), lax.axis_index("mp")
    x, y, z, c = s // 4, s % 4, m // 2, m % 2
    tok_rows = cot.shape[0]
    slots = pt.shape[1]

    def zdev(step, core_step=0):
        return {"dp": s, "mp": (z + step) % 4 * 2 + (c + core_step) % 2}

    def mp_dev(k):
        return {"dp": s, "mp": (m + k) % 8}

    def dp_at(k):
        return (x + OFFSETS[k][0]) % 4 * 4 + (y + OFFSETS[k][1]) % 4

    def remote(src, dst, send_sem, recv_sem, device):
        return pltpu.make_async_remote_copy(
            src_ref=src, dst_ref=dst, send_sem=send_sem, recv_sem=recv_sem,
            device_id=device, device_id_type=MESH,
        )

    def exchange(send, recv, ss, rs):
        return [
            remote(send.at[dp_at(k)], recv.at[s], ss.at[k], rs.at[k], {"dp": dp_at(k), "mp": m})
            for k in range(15)
        ]

    tok_in = pltpu.make_async_copy(tok_hbm, xall.at[m], lsem.at[0])
    cot_in = pltpu.make_async_copy(cot_hbm, cot, lsem.at[1])
    a_in = pltpu.make_async_copy(a_hbm, av, lsem.at[2])
    b_in = pltpu.make_async_copy(b_hbm, bv, lsem.at[3])

    def w_in(j):
        return pltpu.make_async_copy(w_hbm.at[j], wv.at[j], wsem.at[j])

    barrier = pltpu.get_barrier_semaphore()
    for k in range(15):
        pl.semaphore_signal(barrier, inc=1, device_id={"dp": dp_at(k), "mp": m}, device_id_type=MESH)
    for k in range(1, 8):
        pl.semaphore_signal(barrier, inc=1, device_id=mp_dev(k), device_id_type=MESH)
    tok_in.start()
    cot_in.start()
    b_in.start()
    a_in.start()
    for j in range(8):
        w_in(j).start()

    with jax.named_scope("slots"):
        lane = lax.broadcasted_iota(i32, (tok_rows, 128), 1)
        ids = idx_ref[...]
        storage = jnp.sum(
            jnp.where(lane == ids, row_ref[...].astype(f32), 0.0), axis=1, keepdims=True
        )
        hit = (lane.astype(f32) == storage).astype(f32)
        rr = lax.broadcasted_iota(i32, (tok_rows, tok_rows), 0)
        cc = lax.broadcasted_iota(i32, (tok_rows, tok_rows), 1)
        before = dot((cc < rr).astype(f32).astype(bf16), hit.astype(bf16))
        capacity = slots // 128
        dest = storage * capacity + jnp.sum(before * hit, axis=1, keepdims=True)
        dest_row = jnp.sum(jnp.where(rr == cc, dest, 0.0), axis=0, keepdims=True)
        wide = lax.broadcasted_iota(i32, (tok_rows, slots), 1).astype(f32)
        pt[...] = (wide == dest).astype(f32).astype(bf16)
        tall = lax.broadcasted_iota(i32, (slots, tok_rows), 0).astype(f32)
        pm[...] = (tall == dest_row).astype(f32).astype(bf16)

    def place(src, dst):
        def body(i, carry):
            cols = pl.ds(pl.multiple_of(i * 256, 256), 256)
            dst[:, :, cols] = dot(pm[...], src[:, cols]).astype(bf16).reshape(16, 48, 256)
            return carry

        lax.fori_loop(0, 4, body, 0)

    with jax.named_scope("barrier"):
        tok_in.wait()
        pl.semaphore_wait(barrier, 22)

    mine = xall.at[m]
    ag = [
        remote(mine, mine, ag_s.at[0], ag_r.at[0], zdev(1)),
        remote(mine, mine, ag_s.at[1], ag_r.at[1], zdev(3)),
        remote(mine, mine, ag_s.at[2], ag_r.at[2], zdev(0, 1)),
    ]
    for copy in ag:
        copy.start()

    cot_in.wait()
    with jax.named_scope("place_cot"):
        place(cot, sendg)
    g_x = exchange(sendg, recvg, g_s, g_r)
    for copy in g_x:
        copy.start()
    recvg[s] = sendg[s]
    with jax.named_scope("place_tok"):
        place(xall.at[m], sendx)
    recvx[s] = sendx[s]

    def pair(j):
        return remote(part.at[j, :, 1 - c], pr.at[j], p_s.at[j], p_r.at[j], zdev(0, 1))

    def frozen_back(j, carry):
        w_in(j).wait()

        def tile(i, inner):
            cols = pl.ds(pl.multiple_of(i * 256, 256), 256)
            v = dot(cot[...], wv[j, cols, :], NT)
            part[j, :, :, :, cols] = v.astype(bf16).reshape(4, 2, 48, 256)
            return inner

        lax.fori_loop(0, 4, tile, 0)
        pair(j).start()
        return carry

    with jax.named_scope("frozen_back"):
        lax.fori_loop(0, 8, frozen_back, 0)

    x_x = exchange(sendx, recvx, x_s, x_r)
    with jax.named_scope("start_x"):
        for k in range(15):
            g_x[k].wait_send()
            x_x[k].start()

    below, above, far = (z + 3) % 4, (z + 1) % 4, (z + 2) % 4
    lo_rows, hi_rows = pl.ds(0, tok_rows // 2), pl.ds(tok_rows // 2, tok_rows // 2)
    with jax.named_scope("tokens_forward"):
        ag[0].wait_recv()
        from_below, from_above = xall.at[below * 2 + c], xall.at[above * 2 + c]
        far_lo, far_hi = xall.at[far * 2 + c, lo_rows], xall.at[far * 2 + c, hi_rows]
        ag2 = [
            remote(from_below.at[lo_rows], from_below.at[lo_rows], ag_s.at[3], ag_r.at[3], zdev(1)),
            remote(from_above.at[hi_rows], from_above.at[hi_rows], ag_s.at[4], ag_r.at[4], zdev(3)),
            remote(from_below, from_below, ag_s.at[5], ag_r.at[5], zdev(0, 1)),
            remote(from_above, from_above, ag_s.at[6], ag_r.at[6], zdev(0, 1)),
            remote(far_lo, far_lo, ag_s.at[7], ag_r.at[7], zdev(0, 1)),
            remote(far_hi, far_hi, ag_s.at[8], ag_r.at[8], zdev(0, 1)),
        ]
        ag2[0].start()
        ag2[2].start()
        ag[1].wait_recv()
        ag2[1].start()
        ag2[3].start()

    row48 = lax.broadcasted_iota(i32, (48, 512), 0)
    first = (lax.broadcasted_iota(i32, (48, 512), 1) >> 6) * capacity
    keep = ((row48 >= first) & (row48 < first + capacity))[None]

    def project(recv, factor, vs):
        total = None
        for h in range(2):
            v = dot(recv[pl.ds(8 * h, 8)].reshape(384, 1024), factor[...], NT)
            v = jnp.where(keep, v.reshape(8, 48, 512), 0.0).astype(bf16).reshape(384, 512)
            r = lax.broadcasted_iota(i32, (512, 128), 0) & 63
            q = lax.broadcasted_iota(i32, (512, 128), 1)
            v = dot(v, (q == r + 64 * h).astype(f32).astype(bf16))
            total = v if total is None else total + v
        vs[...] = total.astype(bf16).reshape(8, 48, 128)

    def spread(fin, d):
        for h in range(2):
            q = lax.broadcasted_iota(i32, (128, 512), 0)
            r = lax.broadcasted_iota(i32, (128, 512), 1) & 63
            v = dot(fin[...].reshape(384, 128), (q == r + 64 * h).astype(f32).astype(bf16))
            v = jnp.where(keep, v.reshape(8, 48, 512), 0.0).astype(bf16)
            d[pl.ds(h * 384, 384), :] = v.reshape(384, 512)

    def rank_scatter(vs, vr, ss, rs):
        return [
            remote(vs.at[(m + k) % 8], vr.at[m], ss.at[k - 1], rs.at[k - 1], mp_dev(k))
            for k in range(1, 8)
        ]

    def rank_gather(fin, ss, rs):
        return [
            remote(fin.at[m], fin.at[m], ss.at[k + 6], rs.at[k + 6], mp_dev(k)) for k in range(1, 8)
        ]

    def rank_sum(vs, vr, fin):
        vr[m] = vs[m]
        fin[m] = jnp.sum(vr[...].astype(f32), axis=0).astype(bf16)

    b_in.wait()
    with jax.named_scope("wait_g"):
        for copy in g_x:
            copy.wait_recv()
    with jax.named_scope("project_g"):
        project(recvg, bv, vsg)
    g1 = rank_scatter(vsg, vrg, agr_s, agr_r)
    for copy in g1:
        copy.start()

    def pair_sum(j, carry):
        pair(j).wait_recv()
        for q in range(4):
            part[j, q, c] = (part[j, q, c].astype(f32) + pr[j, q].astype(f32)).astype(bf16)
        return carry

    with jax.named_scope("pair_sum"):
        lax.fori_loop(0, 8, pair_sum, 0)
    lo, hi = pl.ds(0, 4), pl.ds(4, 4)
    zc = [
        remote(part.at[lo, far, c], r1.at[lo], z_s.at[0], z_r.at[0], zdev(1)),
        remote(part.at[hi, far, c], r1.at[hi], z_s.at[1], z_r.at[1], zdev(3)),
        remote(part.at[hi, above, c], r2m.at[hi], z_s.at[2], z_r.at[2], zdev(1)),
        remote(part.at[lo, below, c], r2p.at[lo], z_s.at[3], z_r.at[3], zdev(3)),
        remote(part.at[lo, above, c], r2m.at[lo], z_s.at[4], z_r.at[4], zdev(1)),
        remote(part.at[hi, below, c], r2p.at[hi], z_s.at[5], z_r.at[5], zdev(3)),
    ]
    for copy in zc[:4]:
        copy.start()

    with jax.named_scope("rank_sum_g"):
        for copy in g1:
            copy.wait_recv()
        rank_sum(vsg, vrg, fing)
    g2 = rank_gather(fing, agr_s, agr_r)
    for copy in g2:
        copy.start()

    def forward(slot, start):
        def tile(i, carry):
            cols = pl.ds(pl.multiple_of(i * 256, 256), 256)
            v = dot(xall[slot], wv[slot, :, cols])
            acc[:, cols] = v if start else acc[:, cols] + v
            return carry

        lax.fori_loop(0, 4, tile, 0)

    with jax.named_scope("forward_own"):
        forward(m, True)
        ag[2].wait_recv()
        forward(m + 1 - 2 * c, False)

    a_in.wait()
    with jax.named_scope("wait_rank_g"):
        for copy in g2:
            copy.wait_recv()

    def lora(d, factor, send):
        def tile(i, carry):
            cols = pl.ds(pl.multiple_of(i * 256, 256), 256)
            v = adapter_scale * dot(d[...], factor[:, cols])
            send[:, :, cols] = v.astype(bf16).reshape(16, 48, 256)
            return carry

        lax.fori_loop(0, 4, tile, 0)

    with jax.named_scope("lora_back"):
        spread(fing, dg)
        lora(dg, av, sendg)
    rb = exchange(sendg, retb, rb_s, rb_r)
    with jax.named_scope("start_rb"):
        for k in range(15):
            x_x[k].wait_send()
            rb[k].start()
    retb[s] = sendg[s]

    with jax.named_scope("tokens_far"):
        ag2[0].wait_recv()
        ag2[4].start()
        ag2[1].wait_recv()
        ag2[5].start()

    with jax.named_scope("wait_x"):
        for copy in x_x:
            copy.wait_recv()
    with jax.named_scope("project_x"):
        project(recvx, av, vsx)
    x1 = rank_scatter(vsx, vrx, axr_s, axr_r)
    for copy in x1:
        copy.start()

    with jax.named_scope("ring_second"):
        zc[0].wait_recv()

        def add_lo(j, carry):
            part[j, above, c] = (part[j, above, c].astype(f32) + r1[j].astype(f32)).astype(bf16)
            return carry

        lax.fori_loop(0, 4, add_lo, 0)
        zc[4].start()
        zc[1].wait_recv()

        def add_hi(j, carry):
            part[j, below, c] = (part[j, below, c].astype(f32) + r1[j].astype(f32)).astype(bf16)
            return carry

        lax.fori_loop(4, 8, add_hi, 0)
        zc[5].start()

    with jax.named_scope("rank_sum_x"):
        for copy in x1:
            copy.wait_recv()
        rank_sum(vsx, vrx, finx)
    x2 = rank_gather(finx, axr_s, axr_r)
    for copy in x2:
        copy.start()

    def factor_gradient(d, recv):
        def tile(i, carry):
            cols = pl.ds(pl.multiple_of(i * 256, 256), 256)
            v = dot(d[...], recv[:, :, cols].reshape(768, 256), TN)
            grad[:, cols] = adapter_scale * v
            return carry

        lax.fori_loop(0, 4, tile, 0)

    with jax.named_scope("first_gradient"):
        factor_gradient(dg, recvx)
    da_out = pltpu.make_async_copy(grad, da_hbm, osem.at[0])
    da_out.start()

    with jax.named_scope("wait_rank_x"):
        for copy in x2:
            copy.wait_recv()
    with jax.named_scope("lora_out"):
        spread(finx, dx)
        lora(dx, bv, sendx)
    ro = exchange(sendx, reto, ro_s, ro_r)
    with jax.named_scope("start_ro"):
        for k in range(15):
            rb[k].wait_send()
            ro[k].start()
    reto[s] = sendx[s]

    with jax.named_scope("second_gradient"):
        da_out.wait()
        factor_gradient(dx, recvg)
    db_out = pltpu.make_async_copy(grad, db_hbm, osem.at[1])
    db_out.start()

    with jax.named_scope("forward_rest"):
        ag2[2].wait_recv()
        ag2[3].wait_recv()
        ag2[4].wait_recv()
        ag2[5].wait_recv()

        def rest(k, carry):
            forward((m // 2 * 2 + 2 + k) % 8, False)
            return carry

        lax.fori_loop(0, 6, rest, 0)

    with jax.named_scope("wait_rb"):
        for copy in rb:
            copy.wait_recv()

    with jax.named_scope("pick_back"):

        def pick(i, carry):
            cols = pl.ds(pl.multiple_of(i * 256, 256), 256)
            v = dot(pt[...], retb[:, :, cols].reshape(768, 256))
            lbs[:, :, cols] = v.astype(bf16).reshape(8, 48, 256)
            return carry

        lax.fori_loop(0, 4, pick, 0)
    lb = [
        remote(lbs.at[(m + k) % 8], lbr.at[m], lb_s.at[k - 1], lb_r.at[k - 1], mp_dev(k))
        for k in range(1, 8)
    ]
    for copy in lb:
        copy.start()
    lbr[m] = lbs[m]

    with jax.named_scope("wait_ring"):
        for copy in zc[2:]:
            copy.wait_recv()
    with jax.named_scope("wait_lb"):
        for copy in lb:
            copy.wait_recv()

    with jax.named_scope("input_gradient"):
        for j in range(8):
            v = part[j, z, c].astype(f32) + r2m[j].astype(f32) + r2p[j].astype(f32)
            igb[:, j * 1024 : (j + 1) * 1024] = (v + lbr[j].astype(f32)).astype(bf16)
    ig_out = pltpu.make_async_copy(igb, ig_hbm, osem.at[2])
    ig_out.start()

    with jax.named_scope("wait_ro"):
        for copy in ro:
            copy.wait_recv()
    with jax.named_scope("output"):

        def finish(i, carry):
            cols = pl.ds(pl.multiple_of(i * 256, 256), 256)
            v = dot(pt[...], reto[:, :, cols].reshape(768, 256))
            outb[:, cols] = (acc[:, cols] + v).astype(bf16)
            return carry

        lax.fori_loop(0, 4, finish, 0)
    out_out = pltpu.make_async_copy(outb, out_hbm, osem.at[3])
    out_out.start()

    with jax.named_scope("drain"):
        for copy in ag + ag2 + ro + zc + g1 + g2 + x1 + x2 + lb:
            copy.wait_send()

        def drain(j, carry):
            pair(j).wait_send()
            return carry

        lax.fori_loop(0, 8, drain, 0)
        db_out.wait()
        ig_out.wait()
        out_out.wait()


def local(tokens, cotangent, index, storage_row, weight, first_factors, second_factors):
    tok_rows, cols = tokens.shape
    residents, rank, _ = first_factors.shape
    adapters = storage_row.shape[0]
    slots = adapters * max(2, 2 * tok_rows // adapters)
    per = slots // 16
    own = tok_rows // 8
    wide = residents * rank
    anywhere = pl.BlockSpec(memory_space=pl.ANY)
    vmem = pl.BlockSpec(memory_space=pltpu.VMEM)
    dma = pltpu.SemaphoreType.DMA
    rows = pltpu.VMEM((16, per, cols), bf16)
    blocks = pltpu.VMEM((8, own, cols), bf16)
    ranks = pltpu.VMEM((8, own, 128), bf16)
    output, input_gradient, first_gradient, second_gradient = pl.pallas_call(
        kernel,
        out_shape=(
            jax.ShapeDtypeStruct((tok_rows, cols), bf16),
            jax.ShapeDtypeStruct((own, 8 * cols), bf16),
            jax.ShapeDtypeStruct((wide, cols), f32),
            jax.ShapeDtypeStruct((wide, cols), f32),
        ),
        in_specs=[vmem, vmem] + [anywhere] * 5,
        out_specs=[anywhere] * 4,
        scratch_shapes=[
            pltpu.VMEM((8, cols, cols), bf16),
            pltpu.VMEM((8, tok_rows, cols), bf16),
            pltpu.VMEM((tok_rows, cols), bf16),
            pltpu.VMEM((wide, cols), bf16),
            pltpu.VMEM((wide, cols), bf16),
            pltpu.VMEM((tok_rows, slots), bf16),
            pltpu.VMEM((slots, tok_rows), bf16),
            rows, rows, rows, rows, rows, rows,
            pltpu.VMEM((8, 4, 2, own, cols), bf16),
            pltpu.VMEM((8, 4, own, cols), bf16),
            blocks, blocks, blocks, blocks, blocks,
            ranks, ranks, ranks, ranks, ranks, ranks,
            pltpu.VMEM((slots, wide), bf16),
            pltpu.VMEM((slots, wide), bf16),
            pltpu.VMEM((tok_rows, cols), f32),
            pltpu.VMEM((wide, cols), f32),
            pltpu.VMEM((tok_rows, cols), bf16),
            pltpu.VMEM((own, 8 * cols), bf16),
            dma((8,)), dma((4,)), dma((4,)),
            dma((9,)), dma((9,)),
            dma((15,)), dma((15,)), dma((15,)), dma((15,)),
            dma((15,)), dma((15,)), dma((15,)), dma((15,)),
            dma((8,)), dma((8,)), dma((6,)), dma((6,)),
            dma((14,)), dma((14,)), dma((14,)), dma((14,)),
            dma((7,)), dma((7,)),
        ],
        compiler_params=pltpu.CompilerParams(
            collective_id=0, has_side_effects=True, vmem_limit_bytes=62 * 2**20
        ),
        cost_estimate=pl.CostEstimate(
            flops=20_000_000_000, bytes_accessed=30_000_000, transcendentals=0
        ),
        name="adapter_step",
    )(
        index,
        storage_row.reshape(1, adapters),
        tokens,
        cotangent,
        weight.reshape(8, cols, cols),
        first_factors.reshape(wide, cols),
        second_factors.reshape(wide, cols),
    )
    shape = first_factors.shape
    return output, input_gradient, first_gradient.reshape(shape), second_gradient.reshape(shape)


def solution(mesh):
    in_specs = (
        P("dp", "mp"),
        P("dp", "mp"),
        P("dp", None),
        P(),
        P(None, "mp"),
        P("dp", None, "mp"),
        P("dp", None, "mp"),
    )
    out_specs = (P("dp", "mp"), P(("dp", "mp"), None), P("dp", None, "mp"), P("dp", None, "mp"))
    return jax.shard_map(local, mesh=mesh, in_specs=in_specs, out_specs=out_specs, check_vma=False)
```

```python
import jax
import jax.numpy as jnp
from jax import lax
from jax.experimental import pallas as pl
from jax.experimental.pallas import tpu as pltpu
from jax.sharding import PartitionSpec as P

adapter_scale = 2.0
MESH = pl.DeviceIdType.MESH
bf16, f32, i32 = jnp.bfloat16, jnp.float32, jnp.int32

OFFSETS = (
    (1, 0), (3, 0), (0, 1), (0, 3), (2, 2), (1, 1), (3, 3), (1, 3),
    (3, 1), (2, 0), (0, 2), (2, 1), (1, 2), (2, 3), (3, 2),
)
NT = (((1,), (1,)), ((), ()))
TN = (((0,), (0,)), ((), ()))


def dot(a, b, dims=(((1,), (0,)), ((), ()))):
    return lax.dot_general(a, b, dims, preferred_element_type=f32)


def kernel(
    idx_hbm, row_hbm, tok_hbm, cot_hbm, w_hbm, a_hbm, b_hbm,
    out_hbm, ig_hbm, da_hbm, db_hbm,
    idx_ref, row_ref, wv, xall, cot, av, bv, pt, pm, sendg, sendx, recvg, recvx, retb, reto,
    part, pr, r1, r2m, r2p, lbs, lbr, vsg, vrg, fing, vsx, vrx, finx, dg, dx, acc,
    grad, outb, igb,
    wsem, lsem, osem, ag_s, ag_r, g_s, g_r, x_s, x_r, rb_s, rb_r, ro_s, ro_r,
    p_s, p_r, z_s, z_r, rk_s, rk_r, lb_s, lb_r,
):
    s, m = lax.axis_index("dp"), lax.axis_index("mp")
    x, y, z, c = s // 4, s % 4, m // 2, m % 2
    tok_rows = cot.shape[0]
    slots = pt.shape[1]

    def zdev(step, core_step=0):
        return {"dp": s, "mp": (z + step) % 4 * 2 + (c + core_step) % 2}

    def mp_dev(k):
        return {"dp": s, "mp": (m + k) % 8}

    def dp_at(k):
        return (x + OFFSETS[k][0]) % 4 * 4 + (y + OFFSETS[k][1]) % 4

    def remote(src, dst, send_sem, recv_sem, device):
        return pltpu.make_async_remote_copy(
            src_ref=src, dst_ref=dst, send_sem=send_sem, recv_sem=recv_sem,
            device_id=device, device_id_type=MESH,
        )

    def exchange(send, recv, ss, rs):
        return [
            remote(send.at[dp_at(k)], recv.at[s], ss, rs, {"dp": dp_at(k), "mp": m})
            for k in range(15)
        ]

    def landed(ref, sem):
        pltpu.make_async_copy(ref, ref, sem).wait()

    tok_in = pltpu.make_async_copy(tok_hbm, xall.at[m], lsem.at[0])
    cot_in = pltpu.make_async_copy(cot_hbm, cot, lsem.at[1])
    a_in = pltpu.make_async_copy(a_hbm, av, lsem.at[2])
    idx_in = pltpu.make_async_copy(idx_hbm, idx_ref, lsem.at[4])
    row_in = pltpu.make_async_copy(row_hbm, row_ref, lsem.at[5])
    b_in = pltpu.make_async_copy(b_hbm, bv, lsem.at[3])

    def w_in(j):
        return pltpu.make_async_copy(w_hbm.at[j], wv.at[j], wsem.at[j])

    idx_in.start()
    row_in.start()
    barrier = pltpu.get_barrier_semaphore()
    for k in range(15):
        pl.semaphore_signal(barrier, inc=1, device_id={"dp": dp_at(k), "mp": m}, device_id_type=MESH)
    for k in range(1, 8):
        pl.semaphore_signal(barrier, inc=1, device_id=mp_dev(k), device_id_type=MESH)
    tok_in.start()
    cot_in.start()

    with jax.named_scope("slots"):
        idx_in.wait()
        row_in.wait()
        lane = lax.broadcasted_iota(i32, (tok_rows, 128), 1)
        rr = lax.broadcasted_iota(i32, (tok_rows, tok_rows), 0)
        cc = lax.broadcasted_iota(i32, (tok_rows, tok_rows), 1)
        ids = jnp.sum(
            jnp.where(rr == cc, idx_ref[...].astype(f32), 0.0), axis=1, keepdims=True
        )
        storage = jnp.sum(
            jnp.where(lane.astype(f32) == ids, row_ref[...].astype(f32), 0.0), axis=1, keepdims=True
        )
        hit = (lane.astype(f32) == storage).astype(f32)
        before = dot((cc < rr).astype(f32).astype(bf16), hit.astype(bf16))
        capacity = slots // 128
        dest = storage * capacity + jnp.sum(before * hit, axis=1, keepdims=True)
        dest_row = jnp.sum(jnp.where(rr == cc, dest, 0.0), axis=0, keepdims=True)
        wide = lax.broadcasted_iota(i32, (tok_rows, slots), 1).astype(f32)
        pt[...] = (wide == dest).astype(f32).astype(bf16)
        tall = lax.broadcasted_iota(i32, (slots, tok_rows), 0).astype(f32)
        pm[...] = (tall == dest_row).astype(f32).astype(bf16)

    def place(src, dst):
        def body(i, carry):
            cols = pl.ds(pl.multiple_of(i * 256, 256), 256)
            dst[:, :, cols] = dot(pm[...], src[:, cols]).astype(bf16).reshape(16, 48, 256)
            return carry

        lax.fori_loop(0, 4, body, 0)

    cot_in.wait()
    for j in range(8):
        w_in(j).start()
    b_in.start()
    a_in.start()
    with jax.named_scope("place_cot"):
        place(cot, sendg)
        recvg[s] = sendg[s]
    with jax.named_scope("barrier"):
        tok_in.wait()
        pl.semaphore_wait(barrier, 22)

    mine = xall.at[m]
    ag = [
        remote(mine, mine, ag_s, ag_r.at[0], zdev(1)),
        remote(mine, mine, ag_s, ag_r.at[1], zdev(3)),
        remote(mine, mine, ag_s, ag_r.at[2], zdev(0, 1)),
    ]
    for copy in ag:
        copy.start()


    g_x = exchange(sendg, recvg, g_s, g_r)
    for copy in g_x:
        copy.start()
    with jax.named_scope("place_tok"):
        place(xall.at[m], sendx)
        recvx[s] = sendx[s]

    def pair(j):
        return remote(part.at[j, :, 1 - c], pr.at[j], p_s, p_r, zdev(0, 1))

    def frozen_back(j, carry):
        w_in(j).wait()

        def tile(i, inner):
            cols = pl.ds(pl.multiple_of(i * 256, 256), 256)
            v = dot(cot[...], wv[j, cols, :], NT)
            part[j, :, :, :, cols] = v.astype(bf16).reshape(4, 2, 48, 256)
            return inner

        lax.fori_loop(0, 4, tile, 0)
        pair(j).start()
        return carry

    with jax.named_scope("frozen_back"):
        lax.fori_loop(0, 5, frozen_back, 0)

    x_x = exchange(sendx, recvx, x_s, x_r)
    for copy in x_x:
        copy.start()
    with jax.named_scope("frozen_back_2"):
        lax.fori_loop(5, 8, frozen_back, 0)

    def pair_sum(j, carry):
        for q in range(4):
            part[j, q, c] = (part[j, q, c].astype(f32) + pr[j, q].astype(f32)).astype(bf16)
        return carry

    with jax.named_scope("pair_sum"):
        landed(pr, p_r)
        lax.fori_loop(0, 8, pair_sum, 0)
    def forward(slot, start):
        def tile(i, carry):
            cols = pl.ds(pl.multiple_of(i * 256, 256), 256)
            v = dot(xall[slot], wv[slot, :, cols])
            acc[:, cols] = v if start else acc[:, cols] + v
            return carry

        lax.fori_loop(0, 4, tile, 0)

    with jax.named_scope("forward_own"):
        forward(m, True)
        ag[2].wait_recv()
        forward(m + 1 - 2 * c, False)

    below, above, far = (z + 3) % 4, (z + 1) % 4, (z + 2) % 4
    lo_rows, hi_rows = pl.ds(0, tok_rows // 2), pl.ds(tok_rows // 2, tok_rows // 2)
    row48 = lax.broadcasted_iota(i32, (48, 512), 0)
    first = (lax.broadcasted_iota(i32, (48, 512), 1) >> 6) * capacity
    keep = ((row48 >= first) & (row48 < first + capacity))[None]

    def project(recv, factor, vs):
        total = None
        for h in range(2):
            v = dot(recv[pl.ds(8 * h, 8)].reshape(384, 1024), factor[...], NT)
            v = jnp.where(keep, v.reshape(8, 48, 512), 0.0).astype(bf16).reshape(384, 512)
            r = lax.broadcasted_iota(i32, (512, 128), 0) & 63
            q = lax.broadcasted_iota(i32, (512, 128), 1)
            v = dot(v, (q == r + 64 * h).astype(f32).astype(bf16))
            total = v if total is None else total + v
        vs[...] = total.astype(bf16).reshape(8, 48, 128)

    def spread(fin, d):
        for h in range(2):
            q = lax.broadcasted_iota(i32, (128, 512), 0)
            r = lax.broadcasted_iota(i32, (128, 512), 1) & 63
            v = dot(fin[...].reshape(384, 128), (q == r + 64 * h).astype(f32).astype(bf16))
            v = jnp.where(keep, v.reshape(8, 48, 512), 0.0).astype(bf16)
            d[pl.ds(h * 384, 384), :] = v.reshape(384, 512)

    def rank_scatter(vs, vr, ss, rs):
        return [
            remote(vs.at[(m + k) % 8], vr.at[m], ss, rs, mp_dev(k))
            for k in range(1, 8)
        ]

    def rank_gather(fin, ss, rs):
        return [
            remote(fin.at[m], fin.at[m], ss, rs, mp_dev(k)) for k in range(1, 8)
        ]

    def rank_sum(vs, vr, fin):
        vr[m] = vs[m]
        fin[m] = jnp.sum(vr[...].astype(f32), axis=0).astype(bf16)

    b_in.wait()
    with jax.named_scope("wait_g"):
        landed(recvg.at[pl.ds(0, 15)], g_r)
    with jax.named_scope("project_g"):
        project(recvg, bv, vsg)
    g1 = rank_scatter(vsg, vrg, rk_s, rk_r.at[0])
    for copy in g1:
        copy.start()

    lo, hi = pl.ds(0, 4), pl.ds(4, 4)
    zc = [
        remote(part.at[lo, far, c], r1.at[lo], z_s, z_r.at[0], zdev(1)),
        remote(part.at[hi, far, c], r1.at[hi], z_s, z_r.at[1], zdev(3)),
        remote(part.at[hi, above, c], r2m.at[hi], z_s, z_r.at[2], zdev(1)),
        remote(part.at[lo, below, c], r2p.at[lo], z_s, z_r.at[2], zdev(3)),
        remote(part.at[lo, above, c], r2m.at[lo], z_s, z_r.at[2], zdev(1)),
        remote(part.at[hi, below, c], r2p.at[hi], z_s, z_r.at[2], zdev(3)),
    ]
    with jax.named_scope("tokens_forward"):
        ag[0].wait_recv()
        from_below, from_above = xall.at[below * 2 + c], xall.at[above * 2 + c]
        far_lo, far_hi = xall.at[far * 2 + c, lo_rows], xall.at[far * 2 + c, hi_rows]
        ag2 = [
            remote(from_below.at[lo_rows], from_below.at[lo_rows], ag_s, ag_r.at[3], zdev(1)),
            remote(from_above.at[hi_rows], from_above.at[hi_rows], ag_s, ag_r.at[4], zdev(3)),
            remote(from_below, from_below, ag_s, ag_r.at[5], zdev(0, 1)),
            remote(from_above, from_above, ag_s, ag_r.at[6], zdev(0, 1)),
            remote(far_lo, far_lo, ag_s, ag_r.at[7], zdev(0, 1)),
            remote(far_hi, far_hi, ag_s, ag_r.at[8], zdev(0, 1)),
        ]
        ag2[0].start()
        ag2[2].start()
        ag[1].wait_recv()
        ag2[1].start()
        ag2[3].start()

    with jax.named_scope("rank_sum_g"):
        landed(vrg.at[pl.ds(0, 7)], rk_r.at[0])
        landed(vsg.at[pl.ds(0, 7)], rk_s)
        rank_sum(vsg, vrg, fing)
    g2 = rank_gather(fing, rk_s, rk_r.at[1])
    for copy in g2 + zc[:2]:
        copy.start()

    a_in.wait()
    with jax.named_scope("wait_rank_g"):
        landed(fing.at[pl.ds(0, 7)], rk_r.at[1])
        landed(fing.at[pl.ds(0, 7)], rk_s)

    def lora(d, factor, send):
        def tile(i, carry):
            cols = pl.ds(pl.multiple_of(i * 256, 256), 256)
            v = adapter_scale * dot(d[...], factor[:, cols])
            send[:, :, cols] = v.astype(bf16).reshape(16, 48, 256)
            return carry

        lax.fori_loop(0, 4, tile, 0)

    with jax.named_scope("lora_back"):
        landed(sendg.at[pl.ds(0, 15)], g_s)
        spread(fing, dg)
        lora(dg, av, sendg)
    rb = exchange(sendg, retb, rb_s, rb_r)
    for copy in rb:
        copy.start()
    retb[s] = sendg[s]

    with jax.named_scope("wait_x"):
        landed(recvx.at[pl.ds(0, 15)], x_r)
    with jax.named_scope("project_x"):
        project(recvx, av, vsx)
    x1 = rank_scatter(vsx, vrx, rk_s, rk_r.at[2])
    for copy in x1 + zc[2:4]:
        copy.start()

    with jax.named_scope("tokens_far"):
        ag2[0].wait_recv()
        ag2[4].start()
        ag2[1].wait_recv()
        ag2[5].start()

    with jax.named_scope("forward_below"):
        ag2[2].wait_recv()
        forward(below * 2, False)
        forward(below * 2 + 1, False)

    with jax.named_scope("ring_second"):
        zc[0].wait_recv()

        def add_lo(j, carry):
            part[j, above, c] = (part[j, above, c].astype(f32) + r1[j].astype(f32)).astype(bf16)
            return carry

        lax.fori_loop(0, 4, add_lo, 0)
        zc[1].wait_recv()

        def add_hi(j, carry):
            part[j, below, c] = (part[j, below, c].astype(f32) + r1[j].astype(f32)).astype(bf16)
            return carry

        lax.fori_loop(4, 8, add_hi, 0)

    def factor_gradient(d, recv):
        def tile(i, carry):
            cols = pl.ds(pl.multiple_of(i * 256, 256), 256)
            v = dot(d[...], recv[:, :, cols].reshape(768, 256), TN)
            grad[:, cols] = adapter_scale * v
            return carry

        lax.fori_loop(0, 4, tile, 0)

    with jax.named_scope("forward_above"):
        ag2[3].wait_recv()
        forward(above * 2, False)
        forward(above * 2 + 1, False)

    with jax.named_scope("first_gradient"):
        factor_gradient(dg, recvx)
    da_out = pltpu.make_async_copy(grad, da_hbm, osem.at[0])
    da_out.start()

    with jax.named_scope("rank_sum_x"):
        landed(vrx.at[pl.ds(0, 7)], rk_r.at[2])
        landed(vsx.at[pl.ds(0, 7)], rk_s)
        rank_sum(vsx, vrx, finx)
    x2 = rank_gather(finx, rk_s, rk_r.at[3])
    for copy in x2 + zc[4:]:
        copy.start()

    with jax.named_scope("forward_far"):
        ag2[4].wait_recv()
        ag2[5].wait_recv()
        forward(far * 2, False)
        forward(far * 2 + 1, False)


    with jax.named_scope("wait_rank_x"):
        landed(finx.at[pl.ds(0, 7)], rk_r.at[3])
    with jax.named_scope("lora_out"):
        landed(sendx.at[pl.ds(0, 15)], x_s)
        spread(finx, dx)
        lora(dx, bv, sendx)
    ro = exchange(sendx, reto, ro_s, ro_r)
    for copy in ro:
        copy.start()
    reto[s] = sendx[s]

    with jax.named_scope("second_gradient"):
        da_out.wait()
        factor_gradient(dx, recvg)
    db_out = pltpu.make_async_copy(grad, db_hbm, osem.at[1])
    db_out.start()


    with jax.named_scope("wait_rb"):
        landed(retb.at[pl.ds(0, 15)], rb_r)

    with jax.named_scope("pick_back"):

        def pick(i, carry):
            cols = pl.ds(pl.multiple_of(i * 256, 256), 256)
            v = dot(pt[...], retb[:, :, cols].reshape(768, 256))
            lbs[:, :, cols] = v.astype(bf16).reshape(8, 48, 256)
            return carry

        lax.fori_loop(0, 4, pick, 0)
    lb = [
        remote(lbs.at[(m + k) % 8], lbr.at[m], lb_s, lb_r, mp_dev(k))
        for k in range(1, 8)
    ]
    for copy in lb:
        copy.start()
    lbr[m] = lbs[m]

    with jax.named_scope("wait_ring"):
        landed(part.at[pl.ds(0, 2)], z_r.at[2])
    with jax.named_scope("wait_lb"):
        landed(lbr.at[pl.ds(0, 7)], lb_r)

    with jax.named_scope("input_gradient"):
        for j in range(8):
            v = part[j, z, c].astype(f32) + r2m[j].astype(f32) + r2p[j].astype(f32)
            igb[:, j * 1024 : (j + 1) * 1024] = (v + lbr[j].astype(f32)).astype(bf16)
    ig_out = pltpu.make_async_copy(igb, ig_hbm, osem.at[2])
    ig_out.start()

    with jax.named_scope("wait_ro"):
        landed(reto.at[pl.ds(0, 15)], ro_r)
    with jax.named_scope("output"):

        def finish(i, carry):
            cols = pl.ds(pl.multiple_of(i * 256, 256), 256)
            v = dot(pt[...], reto[:, :, cols].reshape(768, 256))
            outb[:, cols] = (acc[:, cols] + v).astype(bf16)
            pltpu.make_async_copy(outb.at[:, cols], out_hbm.at[:, cols], osem.at[3]).start()
            return carry

        lax.fori_loop(0, 4, finish, 0)

    with jax.named_scope("drain"):
        landed(xall.at[pl.ds(0, 7)], ag_s)
        landed(retb.at[pl.ds(0, 15)], rb_s)
        landed(reto.at[pl.ds(0, 15)], ro_s)
        landed(part.at[pl.ds(0, 3)], z_s)
        landed(vsg.at[pl.ds(0, 7)], rk_s)
        landed(lbs.at[pl.ds(0, 7)], lb_s)
        landed(pr, p_s)
        db_out.wait()
        ig_out.wait()
        landed(outb, osem.at[3])


def hand_over(out, ig, da, db, out_to, ig_to, da_to, db_to, out_v, ig_v, da_v, db_v, sem):
    pieces = []
    for src, via, dst, n in (
        (da, da_v, da_to, 4), (db, db_v, db_to, 4), (out, out_v, out_to, 2), (ig, ig_v, ig_to, 1),
    ):
        rows = src.shape[0] // n
        for h in range(n):
            at = pl.ds(h * rows, rows)
            k = len(pieces)
            pieces.append(
                (
                    pltpu.make_async_copy(src.at[at], via.at[at], sem.at[0, k]),
                    pltpu.make_async_copy(via.at[at], dst.at[at], sem.at[1, k]),
                )
            )
    for come, _ in pieces:
        come.start()
    for come, go in pieces:
        come.wait()
        go.start()
    for _, go in pieces:
        go.wait()


def local(tokens, cotangent, index, storage_row, weight, first_factors, second_factors):
    tok_rows, cols = tokens.shape
    residents, rank, _ = first_factors.shape
    adapters = storage_row.shape[0]
    slots = adapters * max(2, 2 * tok_rows // adapters)
    per = slots // 16
    own = tok_rows // 8
    wide = residents * rank
    anywhere = pl.BlockSpec(memory_space=pl.ANY)
    dma = pltpu.SemaphoreType.DMA
    rows = pltpu.VMEM((16, per, cols), bf16)
    blocks = pltpu.VMEM((8, own, cols), bf16)
    ranks = pltpu.VMEM((8, own, 128), bf16)
    results = pl.pallas_call(
        kernel,
        out_shape=(
            jax.ShapeDtypeStruct((tok_rows, cols), bf16),
            jax.ShapeDtypeStruct((own, 8 * cols), bf16),
            jax.ShapeDtypeStruct((wide, cols), f32),
            jax.ShapeDtypeStruct((wide, cols), f32),
        ),
        in_specs=[anywhere] * 7,
        out_specs=[anywhere] * 4,
        scratch_shapes=[
            pltpu.VMEM((1, tok_rows), i32),
            pltpu.VMEM((1, adapters), i32),
            pltpu.VMEM((8, cols, cols), bf16),
            pltpu.VMEM((8, tok_rows, cols), bf16),
            pltpu.VMEM((tok_rows, cols), bf16),
            pltpu.VMEM((wide, cols), bf16),
            pltpu.VMEM((wide, cols), bf16),
            pltpu.VMEM((tok_rows, slots), bf16),
            pltpu.VMEM((slots, tok_rows), bf16),
            rows, rows, rows, rows, rows, rows,
            pltpu.VMEM((8, 4, 2, own, cols), bf16),
            pltpu.VMEM((8, 4, own, cols), bf16),
            blocks, blocks, blocks, blocks, blocks,
            ranks, ranks, ranks, ranks, ranks, ranks,
            pltpu.VMEM((slots, wide), bf16),
            pltpu.VMEM((slots, wide), bf16),
            pltpu.VMEM((tok_rows, cols), f32),
            pltpu.VMEM((wide, cols), f32),
            pltpu.VMEM((tok_rows, cols), bf16),
            pltpu.VMEM((own, 8 * cols), bf16),
            dma((8,)), dma((6,)), dma((4,)),
            dma, dma((9,)),
            dma, dma, dma, dma, dma, dma, dma, dma,
            dma, dma, dma, dma((3,)),
            dma, dma((4,)),
            dma, dma,
        ],
        compiler_params=pltpu.CompilerParams(
            collective_id=0, has_side_effects=True, vmem_limit_bytes=62 * 2**20
        ),
        cost_estimate=pl.CostEstimate(
            flops=20_000_000_000, bytes_accessed=30_000_000, transcendentals=0
        ),
        name="adapter_step",
    )(
        index.reshape(1, tok_rows),
        storage_row.reshape(1, adapters),
        tokens,
        cotangent,
        weight.reshape(8, cols, cols),
        first_factors.reshape(wide, cols),
        second_factors.reshape(wide, cols),
    )
    output, input_gradient, first_gradient, second_gradient = pl.pallas_call(
        hand_over,
        out_shape=tuple(jax.ShapeDtypeStruct(r.shape, r.dtype) for r in results),
        in_specs=[anywhere] * 4,
        out_specs=[anywhere] * 4,
        scratch_shapes=[pltpu.VMEM(r.shape, r.dtype) for r in results] + [dma((2, 11))],
        compiler_params=pltpu.CompilerParams(vmem_limit_bytes=62 * 2**20),
        name="hand_over",
    )(*results)
    shape = first_factors.shape
    return output, input_gradient, first_gradient.reshape(shape), second_gradient.reshape(shape)


def solution(mesh):
    in_specs = (
        P("dp", "mp"),
        P("dp", "mp"),
        P("dp", None),
        P(),
        P(None, "mp"),
        P("dp", None, "mp"),
        P("dp", None, "mp"),
    )
    out_specs = (P("dp", "mp"), P(("dp", "mp"), None), P("dp", None, "mp"), P("dp", None, "mp"))
    return jax.shard_map(local, mesh=mesh, in_specs=in_specs, out_specs=out_specs, check_vma=False)
```

```python
import jax
import jax.numpy as jnp
from jax import lax
from jax.experimental import pallas as pl
from jax.experimental.pallas import tpu as pltpu
from jax.sharding import PartitionSpec as P

adapter_scale = 2.0
MESH = pl.DeviceIdType.MESH
bf16, f32, i32 = jnp.bfloat16, jnp.float32, jnp.int32

OFFSETS = (
    (1, 0), (3, 0), (0, 1), (0, 3), (2, 2), (1, 1), (3, 3), (1, 3),
    (3, 1), (2, 0), (0, 2), (2, 1), (1, 2), (2, 3), (3, 2),
)
NT = (((1,), (1,)), ((), ()))
TN = (((0,), (0,)), ((), ()))


def dot(a, b, dims=(((1,), (0,)), ((), ()))):
    return lax.dot_general(a, b, dims, preferred_element_type=f32)


def kernel(
    idx_hbm, row_hbm, tok_hbm, cot_hbm, w_hbm, a_hbm, b_hbm,
    outb, igb, da, db,
    idx_ref, row_ref, wv, xall, cot, av, bv, pt, pm, sendg, sendx, recvg, recvx, retb, reto,
    part, pr, r1, r2m, r2p, lbs, lbr, vsg, vrg, fing, vsx, vrx, finx, dg, dx, acc,
    wsem, lsem, ag_s, ag_r, g_s, g_r, x_s, x_r, rb_s, rb_r, ro_s, ro_r,
    p_s, p_r, z_s, z_r, rk_s, rk_r, lb_s, lb_r,
):
    s, m = lax.axis_index("dp"), lax.axis_index("mp")
    x, y, z, c = s // 4, s % 4, m // 2, m % 2
    tok_rows = cot.shape[0]
    slots = pt.shape[1]

    def zdev(step, core_step=0):
        return {"dp": s, "mp": (z + step) % 4 * 2 + (c + core_step) % 2}

    def mp_dev(k):
        return {"dp": s, "mp": (m + k) % 8}

    def dp_at(k):
        return (x + OFFSETS[k][0]) % 4 * 4 + (y + OFFSETS[k][1]) % 4

    def remote(src, dst, send_sem, recv_sem, device):
        return pltpu.make_async_remote_copy(
            src_ref=src, dst_ref=dst, send_sem=send_sem, recv_sem=recv_sem,
            device_id=device, device_id_type=MESH,
        )

    def exchange(send, recv, ss, rs):
        return [
            remote(send.at[dp_at(k)], recv.at[s], ss, rs, {"dp": dp_at(k), "mp": m})
            for k in range(15)
        ]

    def landed(ref, sem):
        pltpu.make_async_copy(ref, ref, sem).wait()

    tok_in = pltpu.make_async_copy(tok_hbm, xall.at[m], lsem.at[0])
    cot_in = pltpu.make_async_copy(cot_hbm, cot, lsem.at[1])
    a_in = pltpu.make_async_copy(a_hbm, av, lsem.at[2])
    idx_in = pltpu.make_async_copy(idx_hbm, idx_ref, lsem.at[4])
    row_in = pltpu.make_async_copy(row_hbm, row_ref, lsem.at[5])
    b_in = pltpu.make_async_copy(b_hbm, bv, lsem.at[3])

    def w_in(j):
        return pltpu.make_async_copy(w_hbm.at[j], wv.at[j], wsem.at[j])

    idx_in.start()
    row_in.start()
    barrier = pltpu.get_barrier_semaphore()
    for k in range(15):
        pl.semaphore_signal(barrier, inc=1, device_id={"dp": dp_at(k), "mp": m}, device_id_type=MESH)
    for k in range(1, 8):
        pl.semaphore_signal(barrier, inc=1, device_id=mp_dev(k), device_id_type=MESH)
    tok_in.start()
    cot_in.start()

    with jax.named_scope("slots"):
        idx_in.wait()
        row_in.wait()
        lane = lax.broadcasted_iota(i32, (tok_rows, 128), 1)
        rr = lax.broadcasted_iota(i32, (tok_rows, tok_rows), 0)
        cc = lax.broadcasted_iota(i32, (tok_rows, tok_rows), 1)
        ids = jnp.sum(
            jnp.where(rr == cc, idx_ref[...].astype(f32), 0.0), axis=1, keepdims=True
        )
        storage = jnp.sum(
            jnp.where(lane.astype(f32) == ids, row_ref[...].astype(f32), 0.0), axis=1, keepdims=True
        )
        hit = (lane.astype(f32) == storage).astype(f32)
        before = dot((cc < rr).astype(f32).astype(bf16), hit.astype(bf16))
        capacity = slots // 128
        dest = storage * capacity + jnp.sum(before * hit, axis=1, keepdims=True)
        dest_row = jnp.sum(jnp.where(rr == cc, dest, 0.0), axis=0, keepdims=True)
        wide = lax.broadcasted_iota(i32, (tok_rows, slots), 1).astype(f32)
        pt[...] = (wide == dest).astype(f32).astype(bf16)
        tall = lax.broadcasted_iota(i32, (slots, tok_rows), 0).astype(f32)
        pm[...] = (tall == dest_row).astype(f32).astype(bf16)

    def place(src, dst):
        def body(i, carry):
            cols = pl.ds(pl.multiple_of(i * 256, 256), 256)
            dst[:, :, cols] = dot(pm[...], src[:, cols]).astype(bf16).reshape(16, 48, 256)
            return carry

        lax.fori_loop(0, 4, body, 0)

    cot_in.wait()
    for j in range(8):
        w_in(j).start()
    b_in.start()
    a_in.start()
    with jax.named_scope("place_cot"):
        place(cot, sendg)
        recvg[s] = sendg[s]
    with jax.named_scope("barrier"):
        tok_in.wait()
        pl.semaphore_wait(barrier, 22)

    mine = xall.at[m]
    ag = [
        remote(mine, mine, ag_s, ag_r.at[0], zdev(1)),
        remote(mine, mine, ag_s, ag_r.at[1], zdev(3)),
        remote(mine, mine, ag_s, ag_r.at[2], zdev(0, 1)),
    ]
    for copy in ag:
        copy.start()


    g_x = exchange(sendg, recvg, g_s, g_r)
    for copy in g_x:
        copy.start()
    with jax.named_scope("place_tok"):
        place(xall.at[m], sendx)
        recvx[s] = sendx[s]

    def pair(j):
        return remote(part.at[j, :, 1 - c], pr.at[j], p_s, p_r, zdev(0, 1))

    def frozen_back(j, carry):
        w_in(j).wait()

        def tile(i, inner):
            cols = pl.ds(pl.multiple_of(i * 256, 256), 256)
            v = dot(cot[...], wv[j, cols, :], NT)
            part[j, :, :, :, cols] = v.astype(bf16).reshape(4, 2, 48, 256)
            return inner

        lax.fori_loop(0, 4, tile, 0)
        pair(j).start()
        return carry

    with jax.named_scope("frozen_back"):
        lax.fori_loop(0, 5, frozen_back, 0)

    x_x = exchange(sendx, recvx, x_s, x_r)
    for copy in x_x:
        copy.start()
    with jax.named_scope("frozen_back_2"):
        lax.fori_loop(5, 8, frozen_back, 0)

    def pair_sum(j, carry):
        for q in range(4):
            part[j, q, c] = (part[j, q, c].astype(f32) + pr[j, q].astype(f32)).astype(bf16)
        return carry

    with jax.named_scope("pair_sum"):
        landed(pr, p_r)
        lax.fori_loop(0, 8, pair_sum, 0)
    below, above, far = (z + 3) % 4, (z + 1) % 4, (z + 2) % 4
    lo, hi = pl.ds(0, 4), pl.ds(4, 4)
    zc = [
        remote(part.at[lo, far, c], r1.at[lo], z_s, z_r.at[0], zdev(1)),
        remote(part.at[hi, far, c], r1.at[hi], z_s, z_r.at[1], zdev(3)),
        remote(part.at[hi, above, c], r2m.at[hi], z_s, z_r.at[2], zdev(1)),
        remote(part.at[lo, below, c], r2p.at[lo], z_s, z_r.at[2], zdev(3)),
        remote(part.at[lo, above, c], r2m.at[lo], z_s, z_r.at[2], zdev(1)),
        remote(part.at[hi, below, c], r2p.at[hi], z_s, z_r.at[2], zdev(3)),
    ]
    for copy in zc[:2]:
        copy.start()

    def forward(slot, start):
        def tile(i, carry):
            cols = pl.ds(pl.multiple_of(i * 256, 256), 256)
            v = dot(xall[slot], wv[slot, :, cols])
            acc[:, cols] = v if start else acc[:, cols] + v
            return carry

        lax.fori_loop(0, 4, tile, 0)

    with jax.named_scope("forward_own"):
        forward(m, True)
        ag[2].wait_recv()
        forward(m + 1 - 2 * c, False)

    lo_rows, hi_rows = pl.ds(0, tok_rows // 2), pl.ds(tok_rows // 2, tok_rows // 2)
    row48 = lax.broadcasted_iota(i32, (48, 512), 0)
    first = (lax.broadcasted_iota(i32, (48, 512), 1) >> 6) * capacity
    keep = ((row48 >= first) & (row48 < first + capacity))[None]

    def project(recv, factor, vs):
        total = None
        for h in range(2):
            v = dot(recv[pl.ds(8 * h, 8)].reshape(384, 1024), factor[...], NT)
            v = jnp.where(keep, v.reshape(8, 48, 512), 0.0).astype(bf16).reshape(384, 512)
            r = lax.broadcasted_iota(i32, (512, 128), 0) & 63
            q = lax.broadcasted_iota(i32, (512, 128), 1)
            v = dot(v, (q == r + 64 * h).astype(f32).astype(bf16))
            total = v if total is None else total + v
        vs[...] = total.astype(bf16).reshape(8, 48, 128)

    def spread(fin, d):
        for h in range(2):
            q = lax.broadcasted_iota(i32, (128, 512), 0)
            r = lax.broadcasted_iota(i32, (128, 512), 1) & 63
            v = dot(fin[...].reshape(384, 128), (q == r + 64 * h).astype(f32).astype(bf16))
            v = jnp.where(keep, v.reshape(8, 48, 512), 0.0).astype(bf16)
            d[pl.ds(h * 384, 384), :] = v.reshape(384, 512)

    def rank_scatter(vs, vr, ss, rs):
        return [
            remote(vs.at[(m + k) % 8], vr.at[m], ss, rs, mp_dev(k))
            for k in range(1, 8)
        ]

    def rank_gather(fin, ss, rs):
        return [
            remote(fin.at[m], fin.at[m], ss, rs, mp_dev(k)) for k in range(1, 8)
        ]

    def rank_sum(vs, vr, fin):
        vr[m] = vs[m]
        fin[m] = jnp.sum(vr[...].astype(f32), axis=0).astype(bf16)

    b_in.wait()
    with jax.named_scope("wait_g"):
        landed(recvg.at[pl.ds(0, 15)], g_r)
    with jax.named_scope("project_g"):
        project(recvg, bv, vsg)
    g1 = rank_scatter(vsg, vrg, rk_s, rk_r.at[0])
    for copy in g1:
        copy.start()

    with jax.named_scope("rank_sum_g"):
        landed(vrg.at[pl.ds(0, 7)], rk_r.at[0])
        landed(vsg.at[pl.ds(0, 7)], rk_s)
        rank_sum(vsg, vrg, fing)
    g2 = rank_gather(fing, rk_s, rk_r.at[1])
    for copy in g2:
        copy.start()

    with jax.named_scope("tokens_forward"):
        ag[0].wait_recv()
        from_below, from_above = xall.at[below * 2 + c], xall.at[above * 2 + c]
        far_lo, far_hi = xall.at[far * 2 + c, lo_rows], xall.at[far * 2 + c, hi_rows]
        ag2 = [
            remote(from_below.at[lo_rows], from_below.at[lo_rows], ag_s, ag_r.at[3], zdev(1)),
            remote(from_above.at[hi_rows], from_above.at[hi_rows], ag_s, ag_r.at[4], zdev(3)),
            remote(from_below, from_below, ag_s, ag_r.at[5], zdev(0, 1)),
            remote(from_above, from_above, ag_s, ag_r.at[6], zdev(0, 1)),
            remote(far_lo, far_lo, ag_s, ag_r.at[7], zdev(0, 1)),
            remote(far_hi, far_hi, ag_s, ag_r.at[8], zdev(0, 1)),
        ]
        ag2[0].start()
        ag2[2].start()
        ag[1].wait_recv()
        ag2[1].start()
        ag2[3].start()


    a_in.wait()
    with jax.named_scope("wait_rank_g"):
        landed(fing.at[pl.ds(0, 7)], rk_r.at[1])
        landed(fing.at[pl.ds(0, 7)], rk_s)

    def lora(d, factor, send):
        def tile(i, carry):
            cols = pl.ds(pl.multiple_of(i * 256, 256), 256)
            v = adapter_scale * dot(d[...], factor[:, cols])
            send[:, :, cols] = v.astype(bf16).reshape(16, 48, 256)
            return carry

        lax.fori_loop(0, 4, tile, 0)

    with jax.named_scope("lora_back"):
        landed(sendg.at[pl.ds(0, 15)], g_s)
        spread(fing, dg)
        lora(dg, av, sendg)
    rb = exchange(sendg, retb, rb_s, rb_r)
    for copy in rb:
        copy.start()
    retb[s] = sendg[s]

    with jax.named_scope("wait_x"):
        landed(recvx.at[pl.ds(0, 15)], x_r)
    with jax.named_scope("project_x"):
        project(recvx, av, vsx)
    x1 = rank_scatter(vsx, vrx, rk_s, rk_r.at[2])
    for copy in x1:
        copy.start()

    def factor_gradient(d, recv, grad):
        def tile(i, carry):
            cols = pl.ds(pl.multiple_of(i * 256, 256), 256)
            v = dot(d[...], recv[:, :, cols].reshape(768, 256), TN)
            grad[:, cols] = adapter_scale * v
            return carry

        lax.fori_loop(0, 4, tile, 0)

    with jax.named_scope("ring_second"):
        zc[0].wait_recv()

        def add_lo(j, carry):
            part[j, above, c] = (part[j, above, c].astype(f32) + r1[j].astype(f32)).astype(bf16)
            return carry

        lax.fori_loop(0, 4, add_lo, 0)
        zc[1].wait_recv()

        def add_hi(j, carry):
            part[j, below, c] = (part[j, below, c].astype(f32) + r1[j].astype(f32)).astype(bf16)
            return carry

        lax.fori_loop(4, 8, add_hi, 0)

    with jax.named_scope("forward_below"):
        ag2[2].wait_recv()
        forward(below * 2, False)
        forward(below * 2 + 1, False)

    with jax.named_scope("rank_sum_x"):
        landed(vrx.at[pl.ds(0, 7)], rk_r.at[2])
        landed(vsx.at[pl.ds(0, 7)], rk_s)
        rank_sum(vsx, vrx, finx)
    x2 = rank_gather(finx, rk_s, rk_r.at[3])
    for copy in x2 + zc[2:]:
        copy.start()

    with jax.named_scope("tokens_far"):
        ag2[0].wait_recv()
        ag2[4].start()
        ag2[1].wait_recv()
        ag2[5].start()

    with jax.named_scope("forward_above"):
        ag2[3].wait_recv()
        forward(above * 2, False)
        forward(above * 2 + 1, False)

    with jax.named_scope("wait_rank_x"):
        landed(finx.at[pl.ds(0, 7)], rk_r.at[3])
    with jax.named_scope("lora_out"):
        landed(sendx.at[pl.ds(0, 15)], x_s)
        spread(finx, dx)
        lora(dx, bv, sendx)
    ro = exchange(sendx, reto, ro_s, ro_r)
    for copy in ro:
        copy.start()
    reto[s] = sendx[s]

    with jax.named_scope("first_gradient"):
        factor_gradient(dg, recvx, da)

    with jax.named_scope("second_gradient"):
        factor_gradient(dx, recvg, db)


    with jax.named_scope("forward_far"):
        ag2[4].wait_recv()
        ag2[5].wait_recv()
        forward(far * 2, False)
        forward(far * 2 + 1, False)


    with jax.named_scope("wait_rb"):
        landed(retb.at[pl.ds(0, 15)], rb_r)

    with jax.named_scope("pick_back"):

        def pick(i, carry):
            cols = pl.ds(pl.multiple_of(i * 256, 256), 256)
            v = dot(pt[...], retb[:, :, cols].reshape(768, 256))
            lbs[:, :, cols] = v.astype(bf16).reshape(8, 48, 256)
            return carry

        lax.fori_loop(0, 4, pick, 0)
    lb = [
        remote(lbs.at[(m + k) % 8], lbr.at[m], lb_s, lb_r, mp_dev(k))
        for k in range(1, 8)
    ]
    for copy in lb:
        copy.start()
    lbr[m] = lbs[m]

    with jax.named_scope("wait_ring"):
        landed(part.at[pl.ds(0, 2)], z_r.at[2])
    with jax.named_scope("wait_lb"):
        landed(lbr.at[pl.ds(0, 7)], lb_r)

    with jax.named_scope("input_gradient"):
        for j in range(8):
            v = part[j, z, c].astype(f32) + r2m[j].astype(f32) + r2p[j].astype(f32)
            igb[:, j * 1024 : (j + 1) * 1024] = (v + lbr[j].astype(f32)).astype(bf16)

    with jax.named_scope("wait_ro"):
        landed(reto.at[pl.ds(0, 15)], ro_r)
    with jax.named_scope("output"):

        def finish(i, carry):
            cols = pl.ds(pl.multiple_of(i * 256, 256), 256)
            v = dot(pt[...], reto[:, :, cols].reshape(768, 256))
            outb[:, cols] = (acc[:, cols] + v).astype(bf16)
            return carry

        lax.fori_loop(0, 4, finish, 0)

    with jax.named_scope("drain"):
        landed(xall.at[pl.ds(0, 7)], ag_s)
        landed(retb.at[pl.ds(0, 15)], rb_s)
        landed(reto.at[pl.ds(0, 15)], ro_s)
        landed(part.at[pl.ds(0, 3)], z_s)
        landed(vsg.at[pl.ds(0, 7)], rk_s)
        landed(lbs.at[pl.ds(0, 7)], lb_s)
        landed(pr, p_s)


def hand_over(out, ig, da, db, out_to, ig_to, da_to, db_to, sem):
    copies = []
    for src, dst, n in ((da, da_to, 4), (db, db_to, 4), (out, out_to, 2), (ig, ig_to, 1)):
        rows = src.shape[0] // n
        for h in range(n):
            at = pl.ds(h * rows, rows)
            copies.append(pltpu.make_async_copy(src.at[at], dst.at[at], sem.at[len(copies)]))
    for copy in copies:
        copy.start()
    for copy in copies:
        copy.wait()


def local(tokens, cotangent, index, storage_row, weight, first_factors, second_factors):
    tok_rows, cols = tokens.shape
    residents, rank, _ = first_factors.shape
    adapters = storage_row.shape[0]
    slots = adapters * max(2, 2 * tok_rows // adapters)
    per = slots // 16
    own = tok_rows // 8
    wide = residents * rank
    anywhere = pl.BlockSpec(memory_space=pl.ANY)
    dma = pltpu.SemaphoreType.DMA
    rows = pltpu.VMEM((16, per, cols), bf16)
    blocks = pltpu.VMEM((8, own, cols), bf16)
    ranks = pltpu.VMEM((8, own, 128), bf16)
    results = pl.pallas_call(
        kernel,
        out_shape=(
            pltpu.VMEM((tok_rows, cols), bf16),
            pltpu.VMEM((own, 8 * cols), bf16),
            pltpu.VMEM((wide, cols), f32),
            pltpu.VMEM((wide, cols), f32),
        ),
        in_specs=[anywhere] * 7,
        out_specs=[pl.BlockSpec(memory_space=pltpu.VMEM)] * 4,
        scratch_shapes=[
            pltpu.VMEM((1, tok_rows), i32),
            pltpu.VMEM((1, adapters), i32),
            pltpu.VMEM((8, cols, cols), bf16),
            pltpu.VMEM((8, tok_rows, cols), bf16),
            pltpu.VMEM((tok_rows, cols), bf16),
            pltpu.VMEM((wide, cols), bf16),
            pltpu.VMEM((wide, cols), bf16),
            pltpu.VMEM((tok_rows, slots), bf16),
            pltpu.VMEM((slots, tok_rows), bf16),
            rows, rows, rows, rows, rows, rows,
            pltpu.VMEM((8, 4, 2, own, cols), bf16),
            pltpu.VMEM((8, 4, own, cols), bf16),
            blocks, blocks, blocks, blocks, blocks,
            ranks, ranks, ranks, ranks, ranks, ranks,
            pltpu.VMEM((slots, wide), bf16),
            pltpu.VMEM((slots, wide), bf16),
            pltpu.VMEM((tok_rows, cols), f32),
            dma((8,)), dma((6,)),
            dma, dma((9,)),
            dma, dma, dma, dma, dma, dma, dma, dma,
            dma, dma, dma, dma((3,)),
            dma, dma((4,)),
            dma, dma,
        ],
        compiler_params=pltpu.CompilerParams(
            collective_id=0, has_side_effects=True, vmem_limit_bytes=56 * 2**20
        ),
        cost_estimate=pl.CostEstimate(
            flops=20_000_000_000, bytes_accessed=30_000_000, transcendentals=0
        ),
        name="adapter_step",
    )(
        index.reshape(1, tok_rows),
        storage_row.reshape(1, adapters),
        tokens,
        cotangent,
        weight.reshape(8, cols, cols),
        first_factors.reshape(wide, cols),
        second_factors.reshape(wide, cols),
    )
    output, input_gradient, first_gradient, second_gradient = pl.pallas_call(
        hand_over,
        out_shape=tuple(jax.ShapeDtypeStruct(r.shape, r.dtype) for r in results),
        in_specs=[pl.BlockSpec(memory_space=pltpu.VMEM)] * 4,
        out_specs=[anywhere] * 4,
        scratch_shapes=[dma((11,))],
        compiler_params=pltpu.CompilerParams(vmem_limit_bytes=16 * 2**20),
        name="hand_over",
    )(*results)
    shape = first_factors.shape
    return output, input_gradient, first_gradient.reshape(shape), second_gradient.reshape(shape)


def solution(mesh):
    in_specs = (
        P("dp", "mp"),
        P("dp", "mp"),
        P("dp", None),
        P(),
        P(None, "mp"),
        P("dp", None, "mp"),
        P("dp", None, "mp"),
    )
    out_specs = (P("dp", "mp"), P(("dp", "mp"), None), P("dp", None, "mp"), P("dp", None, "mp"))
    return jax.shard_map(local, mesh=mesh, in_specs=in_specs, out_specs=out_specs, check_vma=False)
```

```python
import jax
import jax.numpy as jnp
from jax import lax
from jax.experimental import pallas as pl
from jax.experimental.pallas import tpu as pltpu
from jax.sharding import PartitionSpec as P

adapter_scale = 2.0
MESH = pl.DeviceIdType.MESH
bf16, f32, i32 = jnp.bfloat16, jnp.float32, jnp.int32

OFFSETS = (
    (1, 0), (3, 0), (0, 1), (0, 3), (2, 2), (1, 1), (3, 3), (2, 0),
    (0, 2), (1, 3), (3, 1), (2, 1), (1, 2), (2, 3), (3, 2),
)
NT = (((1,), (1,)), ((), ()))
TN = (((0,), (0,)), ((), ()))


def dot(a, b, dims=(((1,), (0,)), ((), ()))):
    return lax.dot_general(a, b, dims, preferred_element_type=f32)


def kernel(
    idx_hbm, row_hbm, tok_hbm, cot_hbm, w_hbm, a_hbm, b_hbm,
    igb, da, db, acc, reto, pt,
    idx_ref, row_ref, wv, xall, cot, av, bv, pm, sendg, sendx, recvg, recvx, retb,
    part, pr, r1, r2m, r2p, lbs, lbx, r3, vsg, vrg, fing, vsx, vrx, finx, dg, dx,
    wsem, lsem, ag_s, ag_r, g_s, g_r, x_s, x_r, rb_s, rb_r, ro_s, ro_r,
    p_s, p_r, z_s, z_r, rk_s, rk_r, lb_s, lb_r,
):
    s, m = lax.axis_index("dp"), lax.axis_index("mp")
    x, y, z, c = s // 4, s % 4, m // 2, m % 2
    tok_rows = cot.shape[0]
    slots = pt.shape[1]

    def zdev(step, core_step=0):
        return {"dp": s, "mp": (z + step) % 4 * 2 + (c + core_step) % 2}

    def mp_dev(k):
        return {"dp": s, "mp": (m + k) % 8}

    def dp_at(k):
        return (x + OFFSETS[k][0]) % 4 * 4 + (y + OFFSETS[k][1]) % 4

    def remote(src, dst, send_sem, recv_sem, device):
        return pltpu.make_async_remote_copy(
            src_ref=src, dst_ref=dst, send_sem=send_sem, recv_sem=recv_sem,
            device_id=device, device_id_type=MESH,
        )

    def exchange(send, recv, ss, rs):
        return [
            remote(
                send.at[dp_at(k), pl.ds(16 * r, 16)], recv.at[s, pl.ds(16 * r, 16)], ss, rs,
                {"dp": dp_at(k), "mp": m},
            )
            for r in range(3)
            for k in range(15)
        ]

    def landed(ref, sem):
        pltpu.make_async_copy(ref, ref, sem).wait()

    tok_in = pltpu.make_async_copy(tok_hbm, xall.at[m], lsem.at[0])
    cot_in = pltpu.make_async_copy(cot_hbm, cot, lsem.at[1])
    a_in = pltpu.make_async_copy(a_hbm, av, lsem.at[2])
    idx_in = pltpu.make_async_copy(idx_hbm, idx_ref, lsem.at[4])
    row_in = pltpu.make_async_copy(row_hbm, row_ref, lsem.at[5])
    b_in = pltpu.make_async_copy(b_hbm, bv, lsem.at[3])

    def w_in(j):
        return pltpu.make_async_copy(w_hbm.at[j], wv.at[j], wsem.at[j])

    idx_in.start()
    row_in.start()
    barrier = pltpu.get_barrier_semaphore()
    for k in range(15):
        pl.semaphore_signal(barrier, inc=1, device_id={"dp": dp_at(k), "mp": m}, device_id_type=MESH)
    for k in range(1, 8):
        pl.semaphore_signal(barrier, inc=1, device_id=mp_dev(k), device_id_type=MESH)
    tok_in.start()
    cot_in.start()

    with jax.named_scope("slots"):
        idx_in.wait()
        row_in.wait()
        lane = lax.broadcasted_iota(i32, (tok_rows, 128), 1)
        rr = lax.broadcasted_iota(i32, (tok_rows, tok_rows), 0)
        cc = lax.broadcasted_iota(i32, (tok_rows, tok_rows), 1)
        ids = jnp.sum(
            jnp.where(rr == cc, idx_ref[...].astype(f32), 0.0), axis=1, keepdims=True
        )
        storage = jnp.sum(
            jnp.where(lane.astype(f32) == ids, row_ref[...].astype(f32), 0.0), axis=1, keepdims=True
        )
        hit = (lane.astype(f32) == storage).astype(f32)
        before = dot((cc < rr).astype(f32).astype(bf16), hit.astype(bf16))
        capacity = slots // 128
        dest = storage * capacity + jnp.sum(before * hit, axis=1, keepdims=True)
        dest_row = jnp.sum(jnp.where(rr == cc, dest, 0.0), axis=0, keepdims=True)
        wide = lax.broadcasted_iota(i32, (tok_rows, slots), 1).astype(f32)
        pt[...] = (wide == dest).astype(f32).astype(bf16)
        tall = lax.broadcasted_iota(i32, (slots, tok_rows), 0).astype(f32)
        pm[...] = (tall == dest_row).astype(f32).astype(bf16)

    def place(src, dst):
        def body(i, carry):
            cols = pl.ds(pl.multiple_of(i * 256, 256), 256)
            dst[:, :, cols] = dot(pm[...], src[:, cols]).astype(bf16).reshape(16, 48, 256)
            return carry

        lax.fori_loop(0, 4, body, 0)

    cot_in.wait()
    for j in range(8):
        w_in(j).start()
    b_in.start()
    a_in.start()
    with jax.named_scope("place_cot"):
        place(cot, sendg)
        recvg[s] = sendg[s]
    with jax.named_scope("barrier"):
        tok_in.wait()
        pl.semaphore_wait(barrier, 22)

    mine = xall.at[m]
    ag = [
        remote(mine, mine, ag_s, ag_r.at[0], zdev(1)),
        remote(mine, mine, ag_s, ag_r.at[1], zdev(3)),
        remote(mine, mine, ag_s, ag_r.at[2], zdev(0, 1)),
    ]
    for copy in ag:
        copy.start()


    g_x = exchange(sendg, recvg, g_s, g_r)
    for copy in g_x:
        copy.start()
    with jax.named_scope("place_tok"):
        place(xall.at[m], sendx)
        recvx[s] = sendx[s]

    def pair(j):
        return remote(part.at[j, :, 1 - c], pr.at[j], p_s, p_r, zdev(0, 1))

    def frozen_back(j, carry):
        w_in(j).wait()

        def tile(i, inner):
            cols = pl.ds(pl.multiple_of(i * 256, 256), 256)
            v = dot(cot[...], wv[j, cols, :], NT)
            part[j, :, :, :, cols] = v.astype(bf16).reshape(4, 2, 48, 256)
            return inner

        lax.fori_loop(0, 4, tile, 0)
        pair(j).start()
        return carry

    with jax.named_scope("frozen_back"):
        lax.fori_loop(0, 7, frozen_back, 0)

    x_x = exchange(sendx, recvx, x_s, x_r)
    for copy in x_x:
        copy.start()
    with jax.named_scope("frozen_back_2"):
        lax.fori_loop(7, 8, frozen_back, 0)

    def pair_sum(j, carry):
        for q in range(4):
            part[j, q, c] = (part[j, q, c].astype(f32) + pr[j, q].astype(f32)).astype(bf16)
        return carry

    with jax.named_scope("pair_sum"):
        landed(pr, p_r)
        lax.fori_loop(0, 8, pair_sum, 0)
    below, above, far = (z + 3) % 4, (z + 1) % 4, (z + 2) % 4
    zfirst = []
    for h in range(2):
        lo, hi = pl.ds(2 * h, 2), pl.ds(4 + 2 * h, 2)
        zfirst.append(remote(part.at[lo, far, c], r1.at[lo], z_s, z_r.at[0], zdev(1)))
        zfirst.append(remote(part.at[hi, far, c], r1.at[hi], z_s, z_r.at[1], zdev(3)))
    zfirst[0].start()
    zfirst[1].start()

    def zsecond(step):
        pair_of = pl.ds((z + step) % 4 * 2, 2)
        return [
            remote(part.at[pair_of, above, c], r2m.at[pair_of], z_s, z_r.at[2], zdev(1)),
            remote(part.at[pair_of, below, c], r2p.at[pair_of], z_s, z_r.at[2], zdev(3)),
        ]

    def forward(slot, start):
        def tile(i, carry):
            cols = pl.ds(pl.multiple_of(i * 256, 256), 256)
            v = dot(xall[slot], wv[slot, :, cols])
            acc[:, cols] = v if start else acc[:, cols] + v
            return carry

        lax.fori_loop(0, 4, tile, 0)

    with jax.named_scope("forward_own"):
        forward(m, True)
        ag[2].wait_recv()
        forward(m + 1 - 2 * c, False)

    lo_rows, hi_rows = pl.ds(0, tok_rows // 2), pl.ds(tok_rows // 2, tok_rows // 2)
    row48 = lax.broadcasted_iota(i32, (48, 512), 0)
    first = (lax.broadcasted_iota(i32, (48, 512), 1) >> 6) * capacity
    keep = ((row48 >= first) & (row48 < first + capacity))[None]

    def project(recv, factor, vs):
        total = None
        for h in range(2):
            v = dot(recv[pl.ds(8 * h, 8)].reshape(384, 1024), factor[...], NT)
            v = jnp.where(keep, v.reshape(8, 48, 512), 0.0).astype(bf16).reshape(384, 512)
            r = lax.broadcasted_iota(i32, (512, 128), 0) & 63
            q = lax.broadcasted_iota(i32, (512, 128), 1)
            v = dot(v, (q == r + 64 * h).astype(f32).astype(bf16))
            total = v if total is None else total + v
        vs[...] = total.astype(bf16).reshape(8, 48, 128)

    def spread(fin, d):
        for h in range(2):
            q = lax.broadcasted_iota(i32, (128, 512), 0)
            r = lax.broadcasted_iota(i32, (128, 512), 1) & 63
            v = dot(fin[...].reshape(384, 128), (q == r + 64 * h).astype(f32).astype(bf16))
            v = jnp.where(keep, v.reshape(8, 48, 512), 0.0).astype(bf16)
            d[pl.ds(h * 384, 384), :] = v.reshape(384, 512)

    def rank_scatter(vs, vr, ss, rs):
        return [
            remote(vs.at[(m + k) % 8], vr.at[m], ss, rs, mp_dev(k))
            for k in range(1, 8)
        ]

    def rank_gather(fin, ss, rs):
        return [
            remote(fin.at[m], fin.at[m], ss, rs, mp_dev(k)) for k in range(1, 8)
        ]

    def rank_sum(vs, vr, fin):
        vr[m] = vs[m]
        fin[m] = jnp.sum(vr[...].astype(f32), axis=0).astype(bf16)

    b_in.wait()
    with jax.named_scope("wait_g"):
        landed(recvg.at[pl.ds(0, 15)], g_r)
    with jax.named_scope("project_g"):
        project(recvg, bv, vsg)
    g1 = rank_scatter(vsg, vrg, rk_s, rk_r.at[0])
    for copy in g1:
        copy.start()

    with jax.named_scope("rank_sum_g"):
        landed(vrg.at[pl.ds(0, 7)], rk_r.at[0])
        landed(vsg.at[pl.ds(0, 7)], rk_s)
        rank_sum(vsg, vrg, fing)
    g2 = rank_gather(fing, rk_s, rk_r.at[1])
    for copy in g2 + zfirst[2:]:
        copy.start()

    with jax.named_scope("tokens_forward"):
        ag[0].wait_recv()
        from_below, from_above = xall.at[below * 2 + c], xall.at[above * 2 + c]
        far_lo, far_hi = xall.at[far * 2 + c, lo_rows], xall.at[far * 2 + c, hi_rows]
        ag2 = [
            remote(from_below.at[lo_rows], from_below.at[lo_rows], ag_s, ag_r.at[3], zdev(1)),
            remote(from_above.at[hi_rows], from_above.at[hi_rows], ag_s, ag_r.at[4], zdev(3)),
            remote(from_below, from_below, ag_s, ag_r.at[5], zdev(0, 1)),
            remote(from_above, from_above, ag_s, ag_r.at[6], zdev(0, 1)),
            remote(far_lo, far_lo, ag_s, ag_r.at[7], zdev(0, 1)),
            remote(far_hi, far_hi, ag_s, ag_r.at[8], zdev(0, 1)),
        ]
        ag2[0].start()
        ag2[2].start()
        ag[1].wait_recv()
        ag2[1].start()
        ag2[3].start()


    a_in.wait()
    with jax.named_scope("wait_rank_g"):
        landed(fing.at[pl.ds(0, 7)], rk_r.at[1])
        landed(fing.at[pl.ds(0, 7)], rk_s)

    def lora(d, factor, send):
        def tile(i, carry):
            cols = pl.ds(pl.multiple_of(i * 256, 256), 256)
            v = adapter_scale * dot(d[...], factor[:, cols])
            send[:, :, cols] = v.astype(bf16).reshape(16, 48, 256)
            return carry

        lax.fori_loop(0, 4, tile, 0)

    with jax.named_scope("lora_back"):
        landed(sendg.at[pl.ds(0, 15)], g_s)
        spread(fing, dg)
        lora(dg, av, sendg)
    rb = exchange(sendg, retb, rb_s, rb_r)
    for copy in rb:
        copy.start()
    retb[s] = sendg[s]

    with jax.named_scope("wait_x"):
        landed(recvx.at[pl.ds(0, 15)], x_r)
    with jax.named_scope("project_x"):
        project(recvx, av, vsx)
    x1 = rank_scatter(vsx, vrx, rk_s, rk_r.at[2])
    for copy in x1:
        copy.start()

    def factor_gradient(d, recv, grad):
        def tile(i, carry):
            cols = pl.ds(pl.multiple_of(i * 256, 256), 256)
            v = dot(d[...], recv[:, :, cols].reshape(768, 256), TN)
            grad[:, cols] = adapter_scale * v
            return carry

        lax.fori_loop(0, 4, tile, 0)

    with jax.named_scope("ring_second"):
        landed(r1.at[pl.ds(0, 4)], z_r.at[0])

        def add_lo(j, carry):
            part[j, above, c] = (part[j, above, c].astype(f32) + r1[j].astype(f32)).astype(bf16)
            return carry

        lax.fori_loop(0, 4, add_lo, 0)
        landed(r1.at[pl.ds(4, 4)], z_r.at[1])

        def add_hi(j, carry):
            part[j, below, c] = (part[j, below, c].astype(f32) + r1[j].astype(f32)).astype(bf16)
            return carry

        lax.fori_loop(4, 8, add_hi, 0)

    with jax.named_scope("forward_below"):
        ag2[2].wait_recv()
        forward(below * 2, False)
        forward(below * 2 + 1, False)

    with jax.named_scope("rank_sum_x"):
        landed(vrx.at[pl.ds(0, 7)], rk_r.at[2])
        landed(vsx.at[pl.ds(0, 7)], rk_s)
        rank_sum(vsx, vrx, finx)
    x2 = rank_gather(finx, rk_s, rk_r.at[3])
    for copy in x2 + zsecond(1) + zsecond(2) + zsecond(3):
        copy.start()

    with jax.named_scope("tokens_far"):
        ag2[0].wait_recv()
        ag2[4].start()
        ag2[1].wait_recv()
        ag2[5].start()

    with jax.named_scope("forward_above"):
        ag2[3].wait_recv()
        forward(above * 2, False)
        forward(above * 2 + 1, False)

    with jax.named_scope("wait_rank_x"):
        landed(finx.at[pl.ds(0, 7)], rk_r.at[3])
    with jax.named_scope("lora_out"):
        landed(sendx.at[pl.ds(0, 15)], x_s)
        spread(finx, dx)
        lora(dx, bv, sendx)
    ro = exchange(sendx, reto, ro_s, ro_r)
    for copy in ro:
        copy.start()
    reto[s] = sendx[s]

    with jax.named_scope("first_gradient"):
        factor_gradient(dg, recvx, da)

    with jax.named_scope("second_gradient"):
        factor_gradient(dx, recvg, db)


    with jax.named_scope("forward_far"):
        ag2[4].wait_recv()
        ag2[5].wait_recv()
        forward(far * 2, False)
        forward(far * 2 + 1, False)


    with jax.named_scope("wait_rb"):
        landed(retb.at[pl.ds(0, 15)], rb_r)

    with jax.named_scope("pick_back"):

        def pick(i, carry):
            cols = pl.ds(pl.multiple_of(i * 256, 256), 256)
            v = dot(pt[...], retb[:, :, cols].reshape(768, 256))
            lbs[:, :, :, cols] = v.astype(bf16).reshape(4, 2, 48, 256)
            return carry

        lax.fori_loop(0, 4, pick, 0)
    across = remote(lbs.at[:, 1 - c], lbx, lb_s, lb_r.at[0], zdev(0, 1))
    across.start()
    own, other = m, m + 1 - 2 * c
    with jax.named_scope("add_back"):
        for q in (z, above, below):
            part[own, q, c] = (part[own, q, c].astype(f32) + lbs[q, c].astype(f32)).astype(bf16)
        landed(lbx, lb_r.at[0])
        for q in (z, above, below):
            part[other, q, c] = (part[other, q, c].astype(f32) + lbx[q].astype(f32)).astype(bf16)
    late = zsecond(0) + [
        remote(lbs.at[far, c], r3.at[c], lb_s, lb_r.at[1], zdev(2)),
        remote(lbx.at[far], r3.at[1 - c], lb_s, lb_r.at[1], zdev(2)),
    ]
    for copy in late:
        copy.start()

    with jax.named_scope("wait_ring"):
        landed(part.at[pl.ds(0, 2)], z_r.at[2])
        landed(r3, lb_r.at[1])

    with jax.named_scope("input_gradient"):
        for h in range(2):
            k = far * 2 + h
            part[k, z, c] = (part[k, z, c].astype(f32) + r3[h].astype(f32)).astype(bf16)
        for j in range(8):
            v = part[j, z, c].astype(f32) + r2m[j].astype(f32) + r2p[j].astype(f32)
            igb[:, j * 1024 : (j + 1) * 1024] = v.astype(bf16)

    with jax.named_scope("wait_ro"):
        landed(reto.at[pl.ds(0, 15)], ro_r)
    with jax.named_scope("drain"):
        landed(xall.at[pl.ds(0, 7)], ag_s)
        landed(retb.at[pl.ds(0, 15)], rb_s)
        landed(reto.at[pl.ds(0, 15)], ro_s)
        landed(part.at[pl.ds(0, 3)], z_s)
        landed(vsg.at[pl.ds(0, 7)], rk_s)
        landed(lbx, lb_s)
        landed(r3, lb_s)
        landed(pr, p_s)


def hand_over(ig, da, db, acc, back, pt, out_to, ig_to, da_to, db_to, out, sem):
    copies = []
    for src, dst, n in ((ig, ig_to, 1), (da, da_to, 4), (db, db_to, 4)):
        rows = src.shape[0] // n
        for h in range(n):
            at = pl.ds(h * rows, rows)
            copies.append(pltpu.make_async_copy(src.at[at], dst.at[at], sem.at[len(copies)]))
    for copy in copies:
        copy.start()
    for i in range(4):
        cols = pl.ds(256 * i, 256)
        v = dot(pt[...], back[:, :, cols].reshape(pt.shape[1], 256))
        out[:, cols] = (acc[:, cols] + v).astype(bf16)
        copy = pltpu.make_async_copy(out.at[:, cols], out_to.at[:, cols], sem.at[len(copies)])
        copy.start()
        copies.append(copy)
    for copy in copies:
        copy.wait()


def local(tokens, cotangent, index, storage_row, weight, first_factors, second_factors):
    tok_rows, cols = tokens.shape
    residents, rank, _ = first_factors.shape
    adapters = storage_row.shape[0]
    slots = adapters * max(2, 2 * tok_rows // adapters)
    per = slots // 16
    own = tok_rows // 8
    wide = residents * rank
    anywhere = pl.BlockSpec(memory_space=pl.ANY)
    vmem = pl.BlockSpec(memory_space=pltpu.VMEM)
    dma = pltpu.SemaphoreType.DMA
    rows = pltpu.VMEM((16, per, cols), bf16)
    blocks = pltpu.VMEM((8, own, cols), bf16)
    ranks = pltpu.VMEM((8, own, 128), bf16)
    results = pl.pallas_call(
        kernel,
        out_shape=(
            pltpu.VMEM((own, 8 * cols), bf16),
            pltpu.VMEM((wide, cols), f32),
            pltpu.VMEM((wide, cols), f32),
            pltpu.VMEM((tok_rows, cols), f32),
            rows,
            pltpu.VMEM((tok_rows, slots), bf16),
        ),
        in_specs=[anywhere] * 7,
        out_specs=[vmem] * 6,
        scratch_shapes=[
            pltpu.VMEM((1, tok_rows), i32),
            pltpu.VMEM((1, adapters), i32),
            pltpu.VMEM((8, cols, cols), bf16),
            pltpu.VMEM((8, tok_rows, cols), bf16),
            pltpu.VMEM((tok_rows, cols), bf16),
            pltpu.VMEM((wide, cols), bf16),
            pltpu.VMEM((wide, cols), bf16),
            pltpu.VMEM((slots, tok_rows), bf16),
            rows, rows, rows, rows, rows,
            pltpu.VMEM((8, 4, 2, own, cols), bf16),
            pltpu.VMEM((8, 4, own, cols), bf16),
            blocks, blocks, blocks,
            pltpu.VMEM((4, 2, own, cols), bf16),
            pltpu.VMEM((4, own, cols), bf16),
            pltpu.VMEM((2, own, cols), bf16),
            ranks, ranks, ranks, ranks, ranks, ranks,
            pltpu.VMEM((slots, wide), bf16),
            pltpu.VMEM((slots, wide), bf16),
            dma((8,)), dma((6,)),
            dma, dma((9,)),
            dma, dma, dma, dma, dma, dma, dma, dma,
            dma, dma, dma, dma((3,)),
            dma, dma((4,)),
            dma, dma((2,)),
        ],
        compiler_params=pltpu.CompilerParams(
            collective_id=0, has_side_effects=True, vmem_limit_bytes=54 * 2**20
        ),
        cost_estimate=pl.CostEstimate(
            flops=20_000_000_000, bytes_accessed=30_000_000, transcendentals=0
        ),
        name="adapter_step",
    )(
        index.reshape(1, tok_rows),
        storage_row.reshape(1, adapters),
        tokens,
        cotangent,
        weight.reshape(8, cols, cols),
        first_factors.reshape(wide, cols),
        second_factors.reshape(wide, cols),
    )
    output, input_gradient, first_gradient, second_gradient = pl.pallas_call(
        hand_over,
        out_shape=(
            jax.ShapeDtypeStruct(tokens.shape, bf16),
            jax.ShapeDtypeStruct((own, 8 * cols), bf16),
            jax.ShapeDtypeStruct((wide, cols), f32),
            jax.ShapeDtypeStruct((wide, cols), f32),
        ),
        in_specs=[vmem] * 6,
        out_specs=[anywhere] * 4,
        scratch_shapes=[pltpu.VMEM(tokens.shape, bf16), dma((13,))],
        compiler_params=pltpu.CompilerParams(vmem_limit_bytes=16 * 2**20),
        name="hand_over",
    )(*results)
    shape = first_factors.shape
    return output, input_gradient, first_gradient.reshape(shape), second_gradient.reshape(shape)


def solution(mesh):
    in_specs = (
        P("dp", "mp"),
        P("dp", "mp"),
        P("dp", None),
        P(),
        P(None, "mp"),
        P("dp", None, "mp"),
        P("dp", None, "mp"),
    )
    out_specs = (P("dp", "mp"), P(("dp", "mp"), None), P("dp", None, "mp"), P("dp", None, "mp"))
    return jax.shard_map(local, mesh=mesh, in_specs=in_specs, out_specs=out_specs, check_vma=False)
```

```python
import jax
import jax.numpy as jnp
from jax import lax
from jax.experimental import pallas as pl
from jax.experimental.pallas import tpu as pltpu
from jax.sharding import PartitionSpec as P

adapter_scale = 2.0
MESH = pl.DeviceIdType.MESH
bf16, f32, i32 = jnp.bfloat16, jnp.float32, jnp.int32

OFFSETS = (
    (1, 0), (3, 0), (0, 1), (0, 3), (2, 2), (1, 1), (3, 3), (2, 0),
    (0, 2), (1, 3), (3, 1), (2, 1), (1, 2), (2, 3), (3, 2),
)
NT = (((1,), (1,)), ((), ()))
TN = (((0,), (0,)), ((), ()))


def dot(a, b, dims=(((1,), (0,)), ((), ()))):
    return lax.dot_general(a, b, dims, preferred_element_type=f32)


def kernel(
    idx_hbm, row_hbm, tok_hbm, cot_hbm, w_hbm, a_hbm, b_hbm,
    igb, da, db, acc, reto, pt,
    idx_ref, row_ref, wv, xall, cot, av, bv, pm, sendg, sendx, recvg, recvx, retb,
    part, pr, r1, r2m, r2p, lbs, lbx, r3, vsg, vrg, fing, vsx, vrx, finx, dg, dx,
    wsem, lsem, ag_s, ag_r, g_s, g_r, x_s, x_r, rb_s, rb_r, ro_s, ro_r,
    p_s, p_r, z_s, z_r, rk_s, rk_r, lb_s, lb_r,
):
    s, m = lax.axis_index("dp"), lax.axis_index("mp")
    x, y, z, c = s // 4, s % 4, m // 2, m % 2
    tok_rows = cot.shape[0]
    slots = pt.shape[1]

    def zdev(step, core_step=0):
        return {"dp": s, "mp": (z + step) % 4 * 2 + (c + core_step) % 2}

    def mp_dev(k):
        return {"dp": s, "mp": (m + k) % 8}

    def dp_at(k):
        return (x + OFFSETS[k][0]) % 4 * 4 + (y + OFFSETS[k][1]) % 4

    def remote(src, dst, send_sem, recv_sem, device):
        return pltpu.make_async_remote_copy(
            src_ref=src, dst_ref=dst, send_sem=send_sem, recv_sem=recv_sem,
            device_id=device, device_id_type=MESH,
        )

    def exchange(send, recv, ss, rs):
        def at(k):
            dx, dy = OFFSETS[k]
            ex, ey = (4 - dx) % 4, (4 - dy) % 4
            return (x + dx + (ex - dx) * c) % 4 * 4 + (y + dy + (ey - dy) * c) % 4

        return [
            remote(
                send.at[at(k), :, pl.ds(256 * r, 256)], recv.at[s, :, pl.ds(256 * r, 256)], ss, rs,
                {"dp": at(k), "mp": m},
            )
            for r in range(4)
            for k in range(15)
        ]

    def landed(ref, sem):
        pltpu.make_async_copy(ref, ref, sem).wait()

    tok_in = pltpu.make_async_copy(tok_hbm, xall.at[m], lsem.at[0])
    cot_in = pltpu.make_async_copy(cot_hbm, cot, lsem.at[1])
    a_in = pltpu.make_async_copy(a_hbm, av, lsem.at[2])
    idx_in = pltpu.make_async_copy(idx_hbm, idx_ref, lsem.at[4])
    row_in = pltpu.make_async_copy(row_hbm, row_ref, lsem.at[5])
    b_in = pltpu.make_async_copy(b_hbm, bv, lsem.at[3])

    def w_in(j):
        return pltpu.make_async_copy(w_hbm.at[j], wv.at[j], wsem.at[j])

    idx_in.start()
    row_in.start()
    barrier = pltpu.get_barrier_semaphore()
    for k in range(15):
        pl.semaphore_signal(barrier, inc=1, device_id={"dp": dp_at(k), "mp": m}, device_id_type=MESH)
    for k in range(1, 8):
        pl.semaphore_signal(barrier, inc=1, device_id=mp_dev(k), device_id_type=MESH)
    tok_in.start()
    cot_in.start()

    with jax.named_scope("slots"):
        idx_in.wait()
        row_in.wait()
        lane = lax.broadcasted_iota(i32, (tok_rows, 128), 1)
        rr = lax.broadcasted_iota(i32, (tok_rows, tok_rows), 0)
        cc = lax.broadcasted_iota(i32, (tok_rows, tok_rows), 1)
        ids = jnp.sum(
            jnp.where(rr == cc, idx_ref[...].astype(f32), 0.0), axis=1, keepdims=True
        )
        storage = jnp.sum(
            jnp.where(lane.astype(f32) == ids, row_ref[...].astype(f32), 0.0), axis=1, keepdims=True
        )
        hit = (lane.astype(f32) == storage).astype(f32)
        before = dot((cc < rr).astype(f32).astype(bf16), hit.astype(bf16))
        capacity = slots // 128
        dest = storage * capacity + jnp.sum(before * hit, axis=1, keepdims=True)
        dest_row = jnp.sum(jnp.where(rr == cc, dest, 0.0), axis=0, keepdims=True)
        tall = lax.broadcasted_iota(i32, (slots, tok_rows), 0).astype(f32)
        pm[...] = (tall == dest_row).astype(f32).astype(bf16)

    def place(src, dst):
        def body(i, carry):
            cols = pl.ds(pl.multiple_of(i * 256, 256), 256)
            dst[:, :, cols] = dot(pm[...], src[:, cols]).astype(bf16).reshape(16, 48, 256)
            return carry

        lax.fori_loop(0, 4, body, 0)

    cot_in.wait()
    for j in range(8):
        w_in(j).start()
    b_in.start()
    a_in.start()
    with jax.named_scope("place_cot"):
        place(cot, sendg)
        recvg[s] = sendg[s]
    with jax.named_scope("barrier"):
        tok_in.wait()
        pl.semaphore_wait(barrier, 22)

    mine = xall.at[m]
    ag = [
        remote(mine, mine, ag_s, ag_r.at[0], zdev(1)),
        remote(mine, mine, ag_s, ag_r.at[1], zdev(3)),
        remote(mine, mine, ag_s, ag_r.at[2], zdev(0, 1)),
    ]
    for copy in ag:
        copy.start()


    g_x = exchange(sendg, recvg, g_s, g_r)
    for copy in g_x:
        copy.start()
    with jax.named_scope("place_tok"):
        place(xall.at[m], sendx)
        wide = lax.broadcasted_iota(i32, (tok_rows, slots), 1).astype(f32)
        pt[...] = (wide == dest).astype(f32).astype(bf16)
        recvx[s] = sendx[s]

    def pair(j):
        return remote(part.at[j, :, 1 - c], pr.at[j], p_s, p_r, zdev(0, 1))

    def frozen_back(j, carry):
        w_in(j).wait()

        def tile(i, inner):
            cols = pl.ds(pl.multiple_of(i * 256, 256), 256)
            v = dot(cot[...], wv[j, cols, :], NT)
            part[j, :, :, :, cols] = v.astype(bf16).reshape(4, 2, 48, 256)
            return inner

        lax.fori_loop(0, 4, tile, 0)
        pair(j).start()
        return carry

    with jax.named_scope("frozen_back"):
        lax.fori_loop(0, 7, frozen_back, 0)

    x_x = exchange(sendx, recvx, x_s, x_r)
    for copy in x_x:
        copy.start()
    with jax.named_scope("frozen_back_2"):
        lax.fori_loop(7, 8, frozen_back, 0)

    def pair_sum(j, carry):
        for q in range(4):
            part[j, q, c] = (part[j, q, c].astype(f32) + pr[j, q].astype(f32)).astype(bf16)
        return carry

    with jax.named_scope("pair_sum"):
        landed(pr, p_r)
        lax.fori_loop(0, 8, pair_sum, 0)
    below, above, far = (z + 3) % 4, (z + 1) % 4, (z + 2) % 4
    zfirst = []
    for h in range(2):
        lo, hi = pl.ds(2 * h, 2), pl.ds(4 + 2 * h, 2)
        zfirst.append(remote(part.at[lo, far, c], r1.at[lo], z_s, z_r.at[0], zdev(1)))
        zfirst.append(remote(part.at[hi, far, c], r1.at[hi], z_s, z_r.at[1], zdev(3)))
    zfirst[0].start()
    zfirst[1].start()

    def zsecond(step):
        pair_of = pl.ds((z + step) % 4 * 2, 2)
        return [
            remote(part.at[pair_of, above, c], r2m.at[pair_of], z_s, z_r.at[2], zdev(1)),
            remote(part.at[pair_of, below, c], r2p.at[pair_of], z_s, z_r.at[2], zdev(3)),
        ]

    def forward(slot, start):
        def tile(i, carry):
            cols = pl.ds(pl.multiple_of(i * 256, 256), 256)
            v = dot(xall[slot], wv[slot, :, cols])
            acc[:, cols] = v if start else acc[:, cols] + v
            return carry

        lax.fori_loop(0, 4, tile, 0)

    with jax.named_scope("forward_own"):
        forward(m, True)
        ag[2].wait_recv()
        forward(m + 1 - 2 * c, False)

    lo_rows, hi_rows = pl.ds(0, tok_rows // 2), pl.ds(tok_rows // 2, tok_rows // 2)
    row48 = lax.broadcasted_iota(i32, (48, 512), 0)
    first = (lax.broadcasted_iota(i32, (48, 512), 1) >> 6) * capacity
    keep = ((row48 >= first) & (row48 < first + capacity))[None]

    def project(recv, factor, vs):
        total = None
        for h in range(2):
            v = dot(recv[pl.ds(8 * h, 8)].reshape(384, 1024), factor[...], NT)
            v = jnp.where(keep, v.reshape(8, 48, 512), 0.0).astype(bf16).reshape(384, 512)
            r = lax.broadcasted_iota(i32, (512, 128), 0) & 63
            q = lax.broadcasted_iota(i32, (512, 128), 1)
            v = dot(v, (q == r + 64 * h).astype(f32).astype(bf16))
            total = v if total is None else total + v
        vs[...] = total.astype(bf16).reshape(8, 48, 128)

    def spread(fin, d):
        for h in range(2):
            q = lax.broadcasted_iota(i32, (128, 512), 0)
            r = lax.broadcasted_iota(i32, (128, 512), 1) & 63
            v = dot(fin[...].reshape(384, 128), (q == r + 64 * h).astype(f32).astype(bf16))
            v = jnp.where(keep, v.reshape(8, 48, 512), 0.0).astype(bf16)
            d[pl.ds(h * 384, 384), :] = v.reshape(384, 512)

    def rank_scatter(vs, vr, ss, rs):
        return [
            remote(vs.at[(m + k) % 8], vr.at[m], ss, rs, mp_dev(k))
            for k in range(1, 8)
        ]

    def rank_gather(fin, ss, rs):
        return [
            remote(fin.at[m], fin.at[m], ss, rs, mp_dev(k)) for k in range(1, 8)
        ]

    def rank_sum(vs, vr, fin):
        vr[m] = vs[m]
        fin[m] = jnp.sum(vr[...].astype(f32), axis=0).astype(bf16)

    b_in.wait()
    with jax.named_scope("wait_g"):
        landed(recvg.at[pl.ds(0, 15)], g_r)
    with jax.named_scope("project_g"):
        project(recvg, bv, vsg)
    g1 = rank_scatter(vsg, vrg, rk_s, rk_r.at[0])
    for copy in g1:
        copy.start()

    with jax.named_scope("rank_sum_g"):
        landed(vrg.at[pl.ds(0, 7)], rk_r.at[0])
        landed(vsg.at[pl.ds(0, 7)], rk_s)
        rank_sum(vsg, vrg, fing)
    g2 = rank_gather(fing, rk_s, rk_r.at[1])
    for copy in g2 + zfirst[2:]:
        copy.start()

    with jax.named_scope("tokens_forward"):
        ag[0].wait_recv()
        from_below, from_above = xall.at[below * 2 + c], xall.at[above * 2 + c]
        far_lo, far_hi = xall.at[far * 2 + c, lo_rows], xall.at[far * 2 + c, hi_rows]
        ag2 = [
            remote(from_below.at[lo_rows], from_below.at[lo_rows], ag_s, ag_r.at[3], zdev(1)),
            remote(from_above.at[hi_rows], from_above.at[hi_rows], ag_s, ag_r.at[4], zdev(3)),
            remote(from_below, from_below, ag_s, ag_r.at[5], zdev(0, 1)),
            remote(from_above, from_above, ag_s, ag_r.at[6], zdev(0, 1)),
            remote(far_lo, far_lo, ag_s, ag_r.at[7], zdev(0, 1)),
            remote(far_hi, far_hi, ag_s, ag_r.at[8], zdev(0, 1)),
        ]
        ag2[0].start()
        ag2[2].start()
        ag[1].wait_recv()
        ag2[1].start()
        ag2[3].start()


    a_in.wait()
    with jax.named_scope("wait_rank_g"):
        landed(fing.at[pl.ds(0, 7)], rk_r.at[1])
        landed(fing.at[pl.ds(0, 7)], rk_s)

    def lora(d, factor, send):
        def tile(i, carry):
            cols = pl.ds(pl.multiple_of(i * 256, 256), 256)
            v = adapter_scale * dot(d[...], factor[:, cols])
            send[:, :, cols] = v.astype(bf16).reshape(16, 48, 256)
            return carry

        lax.fori_loop(0, 4, tile, 0)

    with jax.named_scope("lora_back"):
        landed(sendg.at[pl.ds(0, 15)], g_s)
        spread(fing, dg)
        lora(dg, av, sendg)
    rb = exchange(sendg, retb, rb_s, rb_r)
    for copy in rb:
        copy.start()
    retb[s] = sendg[s]

    with jax.named_scope("wait_x"):
        landed(recvx.at[pl.ds(0, 15)], x_r)
    with jax.named_scope("project_x"):
        project(recvx, av, vsx)
    x1 = rank_scatter(vsx, vrx, rk_s, rk_r.at[2])
    for copy in x1:
        copy.start()

    def factor_gradient(d, recv, grad):
        def tile(i, carry):
            cols = pl.ds(pl.multiple_of(i * 256, 256), 256)
            v = dot(d[...], recv[:, :, cols].reshape(768, 256), TN)
            grad[:, cols] = adapter_scale * v
            return carry

        lax.fori_loop(0, 4, tile, 0)

    with jax.named_scope("ring_second"):
        landed(r1.at[pl.ds(0, 4)], z_r.at[0])

        def add_lo(j, carry):
            part[j, above, c] = (part[j, above, c].astype(f32) + r1[j].astype(f32)).astype(bf16)
            return carry

        lax.fori_loop(0, 4, add_lo, 0)
        landed(r1.at[pl.ds(4, 4)], z_r.at[1])

        def add_hi(j, carry):
            part[j, below, c] = (part[j, below, c].astype(f32) + r1[j].astype(f32)).astype(bf16)
            return carry

        lax.fori_loop(4, 8, add_hi, 0)

    with jax.named_scope("forward_below"):
        ag2[2].wait_recv()
        forward(below * 2, False)
        forward(below * 2 + 1, False)

    with jax.named_scope("rank_sum_x"):
        landed(vrx.at[pl.ds(0, 7)], rk_r.at[2])
        landed(vsx.at[pl.ds(0, 7)], rk_s)
        rank_sum(vsx, vrx, finx)
    x2 = rank_gather(finx, rk_s, rk_r.at[3])
    for copy in x2 + zsecond(1) + zsecond(2) + zsecond(3):
        copy.start()

    with jax.named_scope("tokens_far"):
        ag2[0].wait_recv()
        ag2[4].start()
        ag2[1].wait_recv()
        ag2[5].start()

    with jax.named_scope("forward_above"):
        ag2[3].wait_recv()
        forward(above * 2, False)
        forward(above * 2 + 1, False)

    with jax.named_scope("wait_rank_x"):
        landed(finx.at[pl.ds(0, 7)], rk_r.at[3])
    with jax.named_scope("lora_out"):
        landed(sendx.at[pl.ds(0, 15)], x_s)
        spread(finx, dx)
        lora(dx, bv, sendx)
    ro = exchange(sendx, reto, ro_s, ro_r)
    for copy in ro:
        copy.start()
    reto[s] = sendx[s]

    with jax.named_scope("first_gradient"):
        factor_gradient(dg, recvx, da)

    with jax.named_scope("second_gradient"):
        factor_gradient(dx, recvg, db)


    with jax.named_scope("forward_far"):
        ag2[4].wait_recv()
        ag2[5].wait_recv()
        forward(far * 2, False)
        forward(far * 2 + 1, False)


    with jax.named_scope("wait_rb"):
        landed(retb.at[pl.ds(0, 15)], rb_r)

    with jax.named_scope("pick_back"):

        def pick(i, carry):
            cols = pl.ds(pl.multiple_of(i * 256, 256), 256)
            v = dot(pt[...], retb[:, :, cols].reshape(768, 256))
            lbs[:, :, :, cols] = v.astype(bf16).reshape(4, 2, 48, 256)
            return carry

        lax.fori_loop(0, 4, pick, 0)
    across = remote(lbs.at[:, 1 - c], lbx, lb_s, lb_r.at[0], zdev(0, 1))
    across.start()
    own, other = m, m + 1 - 2 * c
    with jax.named_scope("add_back"):
        for q in (z, above, below):
            part[own, q, c] = (part[own, q, c].astype(f32) + lbs[q, c].astype(f32)).astype(bf16)
        landed(lbx, lb_r.at[0])
        for q in (z, above, below):
            part[other, q, c] = (part[other, q, c].astype(f32) + lbx[q].astype(f32)).astype(bf16)
    late = zsecond(0) + [
        remote(lbs.at[far, c], r3.at[c], lb_s, lb_r.at[1], zdev(2)),
        remote(lbx.at[far], r3.at[1 - c], lb_s, lb_r.at[1], zdev(2)),
    ]
    for copy in late:
        copy.start()

    with jax.named_scope("wait_ring"):
        landed(part.at[pl.ds(0, 2)], z_r.at[2])
        landed(r3, lb_r.at[1])

    with jax.named_scope("input_gradient"):
        for h in range(2):
            k = far * 2 + h
            part[k, z, c] = (part[k, z, c].astype(f32) + r3[h].astype(f32)).astype(bf16)
        for j in range(8):
            v = part[j, z, c].astype(f32) + r2m[j].astype(f32) + r2p[j].astype(f32)
            igb[:, j * 1024 : (j + 1) * 1024] = v.astype(bf16)

    with jax.named_scope("wait_ro"):
        landed(reto.at[pl.ds(0, 15)], ro_r)
    with jax.named_scope("drain"):
        landed(xall.at[pl.ds(0, 7)], ag_s)
        landed(retb.at[pl.ds(0, 15)], rb_s)
        landed(reto.at[pl.ds(0, 15)], ro_s)
        landed(part.at[pl.ds(0, 3)], z_s)
        landed(vsg.at[pl.ds(0, 7)], rk_s)
        landed(lbx, lb_s)
        landed(r3, lb_s)
        landed(pr, p_s)


def hand_over(ig, da, db, acc, back, pt, out_to, ig_to, da_to, db_to, out, sem):
    copies = []
    for src, dst, n in ((ig, ig_to, 1), (da, da_to, 4), (db, db_to, 4)):
        rows = src.shape[0] // n
        for h in range(n):
            at = pl.ds(h * rows, rows)
            copies.append(pltpu.make_async_copy(src.at[at], dst.at[at], sem.at[len(copies)]))
    for copy in copies:
        copy.start()
    for i in range(4):
        cols = pl.ds(256 * i, 256)
        v = dot(pt[...], back[:, :, cols].reshape(pt.shape[1], 256))
        out[:, cols] = (acc[:, cols] + v).astype(bf16)
        copy = pltpu.make_async_copy(out.at[:, cols], out_to.at[:, cols], sem.at[len(copies)])
        copy.start()
        copies.append(copy)
    for copy in copies:
        copy.wait()


def local(tokens, cotangent, index, storage_row, weight, first_factors, second_factors):
    tok_rows, cols = tokens.shape
    residents, rank, _ = first_factors.shape
    adapters = storage_row.shape[0]
    slots = adapters * max(2, 2 * tok_rows // adapters)
    per = slots // 16
    own = tok_rows // 8
    wide = residents * rank
    anywhere = pl.BlockSpec(memory_space=pl.ANY)
    vmem = pl.BlockSpec(memory_space=pltpu.VMEM)
    dma = pltpu.SemaphoreType.DMA
    rows = pltpu.VMEM((16, per, cols), bf16)
    blocks = pltpu.VMEM((8, own, cols), bf16)
    ranks = pltpu.VMEM((8, own, 128), bf16)
    results = pl.pallas_call(
        kernel,
        out_shape=(
            pltpu.VMEM((own, 8 * cols), bf16),
            pltpu.VMEM((wide, cols), f32),
            pltpu.VMEM((wide, cols), f32),
            pltpu.VMEM((tok_rows, cols), f32),
            rows,
            pltpu.VMEM((tok_rows, slots), bf16),
        ),
        in_specs=[anywhere] * 7,
        out_specs=[vmem] * 6,
        scratch_shapes=[
            pltpu.VMEM((1, tok_rows), i32),
            pltpu.VMEM((1, adapters), i32),
            pltpu.VMEM((8, cols, cols), bf16),
            pltpu.VMEM((8, tok_rows, cols), bf16),
            pltpu.VMEM((tok_rows, cols), bf16),
            pltpu.VMEM((wide, cols), bf16),
            pltpu.VMEM((wide, cols), bf16),
            pltpu.VMEM((slots, tok_rows), bf16),
            rows, rows, rows, rows, rows,
            pltpu.VMEM((8, 4, 2, own, cols), bf16),
            pltpu.VMEM((8, 4, own, cols), bf16),
            blocks, blocks, blocks,
            pltpu.VMEM((4, 2, own, cols), bf16),
            pltpu.VMEM((4, own, cols), bf16),
            pltpu.VMEM((2, own, cols), bf16),
            ranks, ranks, ranks, ranks, ranks, ranks,
            pltpu.VMEM((slots, wide), bf16),
            pltpu.VMEM((slots, wide), bf16),
            dma((8,)), dma((6,)),
            dma, dma((9,)),
            dma, dma, dma, dma, dma, dma, dma, dma,
            dma, dma, dma, dma((3,)),
            dma, dma((4,)),
            dma, dma((2,)),
        ],
        compiler_params=pltpu.CompilerParams(
            collective_id=0, has_side_effects=True, vmem_limit_bytes=54 * 2**20
        ),
        cost_estimate=pl.CostEstimate(
            flops=20_000_000_000, bytes_accessed=30_000_000, transcendentals=0
        ),
        name="adapter_step",
    )(
        index.reshape(1, tok_rows),
        storage_row.reshape(1, adapters),
        tokens,
        cotangent,
        weight.reshape(8, cols, cols),
        first_factors.reshape(wide, cols),
        second_factors.reshape(wide, cols),
    )
    output, input_gradient, first_gradient, second_gradient = pl.pallas_call(
        hand_over,
        out_shape=(
            jax.ShapeDtypeStruct(tokens.shape, bf16),
            jax.ShapeDtypeStruct((own, 8 * cols), bf16),
            jax.ShapeDtypeStruct((wide, cols), f32),
            jax.ShapeDtypeStruct((wide, cols), f32),
        ),
        in_specs=[vmem] * 6,
        out_specs=[anywhere] * 4,
        scratch_shapes=[pltpu.VMEM(tokens.shape, bf16), dma((13,))],
        compiler_params=pltpu.CompilerParams(vmem_limit_bytes=16 * 2**20),
        name="hand_over",
    )(*results)
    shape = first_factors.shape
    return output, input_gradient, first_gradient.reshape(shape), second_gradient.reshape(shape)


def solution(mesh):
    in_specs = (
        P("dp", "mp"),
        P("dp", "mp"),
        P("dp", None),
        P(),
        P(None, "mp"),
        P("dp", None, "mp"),
        P("dp", None, "mp"),
    )
    out_specs = (P("dp", "mp"), P(("dp", "mp"), None), P("dp", None, "mp"), P("dp", None, "mp"))
    return jax.shard_map(local, mesh=mesh, in_specs=in_specs, out_specs=out_specs, check_vma=False)
```
